256 devices in a mesh: wide: 32 (over x, z), narrow: 8 (over y, core).
Axes of the slice: x: 4, y: 4, z: 8, core: 2. Of those that a mesh axis runs over, the one named last changes fastest.
Arguments:
- tokens: bfloat16 [65536, 4096], P(('wide', 'narrow')), may hold values from -6 to 6
- block_scales: float32 [65536, 32], P(('wide', 'narrow')), may hold values from 0.5 to 2
- pick_index: int32 [32, 384], replicated, may hold values from 0 to 65535, as said below
- pick_gates: float32 [32, 384], replicated, may hold values from 0.1 to 1
- pick_counts: int32 [65536], P(('wide', 'narrow')), may hold values from 0 to 32, as said below
- gate_weight: bfloat16 [32, 4096, 1536], P('wide', None, 'narrow'), may hold values from -0.09375 to 0.09375
- up_weight: bfloat16 [32, 4096, 1536], P('wide', None, 'narrow'), may hold values from -0.09375 to 0.09375
- down_weight: bfloat16 [32, 1536, 4096], P('wide', 'narrow'), may hold values from -0.15625 to 0.15625
Outputs:
- mixed: bfloat16 [65536, 4096], P(('wide', 'narrow'))
The draws below stay inside these ranges and needn't reach their ends.
Inputs may be any that keep to these rules, and one draw needn't show every extreme that they name: `pick_index`: each row names 384 different tokens; at most 3 of them lie among the 256 tokens of one device (tokens d * 256 to (d + 1) * 256 - 1), and in every row some device has exactly 3. `pick_counts`: the number of times the token appears in pick_index.
All inputs are finite; a program needn't handle non-finite values.
Results may differ from the reference program's by a relative error of at most 0.0041.
Values may be sent and summed in bfloat16 or wider, within the bound.
No kernel may reach another device: no remote copies, remote signals or barrier semaphores. Data moves between devices by JAX's collectives and lax.ppermute only.
A program may use at most 128 MiB of HBM per device.

```python
import math
import jax
import jax.numpy as jnp
from jax import lax

D = 4096
HIDDEN_SIZE = 1536
BLOCK = 128
MOST = 3
TOK_DEV = 256
EXPERTS = 32
TOKENS = 65536
CAP = 384
DEVICES = 256


def make_picks(key):

    def one_expert(expert):
        sub_key = jax.random.fold_in(key, expert)
        key_order, key_split, key_tokens, key_shuffle = jax.random.split(sub_key, 4)
        order = jax.random.permutation(key_order, DEVICES).astype(jnp.int32)
        where_zero = jnp.argmax(order == 0).astype(jnp.int32)
        first = order[0]
        order = order.at[where_zero].set(first).at[0].set(0)
        shares = jax.random.randint(key_split, (DEVICES // 2,), 0, MOST + 1)
        shares = shares.at[0].set(MOST)
        per_device = jnp.zeros((DEVICES,), jnp.int32)
        per_device = per_device.at[order[0::2]].set(shares)
        per_device = per_device.at[order[1::2]].set(MOST - shares)
        scores = jax.random.randint(key_tokens, (DEVICES, TOK_DEV), 0, 65536)
        scores = scores * TOK_DEV + jnp.arange(TOK_DEV, dtype=jnp.int32)[None, :]
        scores = scores.at[0, 0].set(-1)
        ranked = jnp.argsort(scores, axis=1).astype(jnp.int32)
        offsets = (jnp.arange(DEVICES, dtype=jnp.int32) * TOK_DEV)[:, None]
        candidate = (ranked[:, :MOST] + offsets).reshape(-1)
        valid = (jnp.arange(MOST, dtype=jnp.int32)[None, :] < per_device[:, None]).reshape(-1)
        position = jnp.arange(DEVICES * MOST, dtype=jnp.int32)
        sort_keys = jnp.where(valid, position, position + DEVICES * MOST)
        chosen = jnp.argsort(sort_keys).astype(jnp.int32)[:CAP]
        picks = candidate[chosen]
        shuffle = jax.random.permutation(key_shuffle, CAP)
        return picks[shuffle]
    return lax.map(one_expert, jnp.arange(EXPERTS, dtype=jnp.int32))


def draw_pick_index(key, part):
    return make_picks(key).astype(jnp.int32)


def draw_pick_counts(key, part):
    picks = make_picks(key)
    return jnp.zeros((TOKENS,), jnp.int32).at[picks.reshape(-1)].add(1)


def shard_levels(rng, extent, cuts, least, top_value):
    def one(axis_at, blocks):
        steps = jax.random.uniform(jax.random.fold_in(jax.random.fold_in(rng, 6), axis_at), (blocks,), jnp.float32, least / len(cuts), top_value / len(cuts))
        return jnp.repeat(jnp.exp(steps), extent[axis_at] // blocks).reshape((-1,) + (1,) * (len(extent) - axis_at - 1))

    level = one(*cuts[0])
    for cut in cuts[1:]:
        level = level * one(*cut)
    return level


def normal_values(stream_key, dims, spread, reach, cuts=(), held_as=jnp.bfloat16):
    array = spread * jax.random.normal(stream_key, dims, jnp.float32)
    if cuts:
        array = array * shard_levels(stream_key, dims, cuts, -0.22, 0.18)
    return jnp.clip(array, -reach, reach).astype(held_as)


def setup_inputs(seed: int = 0) -> dict:
    arg_keys = jax.random.split(jax.random.key(seed), 9)
    tokens = normal_values(arg_keys[0], (TOKENS, D), 1.0, 6.0, ((0, 256),))
    block_scales = jnp.clip(jnp.exp(math.log(2.0) - 1.3862944 * jax.random.uniform(arg_keys[1], (TOKENS, D // BLOCK), jnp.float32) ** shard_levels(arg_keys[1], (TOKENS, D // BLOCK), ((0, 256),), -0.2, 0.2)), 0.5, 2.0)
    pick_index = draw_pick_index(jax.random.fold_in(arg_keys[8], 71), 0)
    pick_gates = jnp.clip(jnp.exp(jax.random.uniform(arg_keys[3], (EXPERTS, CAP), jnp.float32, math.log(0.1), math.log(1.0))), 0.1, 1.0)
    pick_counts = draw_pick_counts(jax.random.fold_in(arg_keys[8], 71), 0)
    gate_weight = normal_values(arg_keys[5], (EXPERTS, D, HIDDEN_SIZE), D ** -0.5, 0.09375, ((0, 32), (2, 8)))
    up_weight = normal_values(arg_keys[6], (EXPERTS, D, HIDDEN_SIZE), D ** -0.5, 0.09375, ((0, 32), (2, 8)))
    down_weight = normal_values(arg_keys[7], (EXPERTS, HIDDEN_SIZE, D), HIDDEN_SIZE ** -0.5, 0.15625, ((0, 32), (1, 8)))
    return {"tokens": tokens, "block_scales": block_scales, "pick_index": pick_index, "pick_gates": pick_gates, "pick_counts": pick_counts, "gate_weight": gate_weight, "up_weight": up_weight, "down_weight": down_weight}


def reference(tokens, block_scales, pick_index, pick_gates, pick_counts, gate_weight, up_weight, down_weight):
    scaled = tokens.astype(jnp.float32).reshape(TOKENS, D // BLOCK, BLOCK) * block_scales[:, :, None]
    rows = scaled.reshape(TOKENS, D).astype(jnp.bfloat16)

    def one_expert(expert):
        picked = rows[pick_index[expert]]
        gate = jnp.dot(picked, gate_weight[expert], preferred_element_type=jnp.float32)
        upper = jnp.dot(picked, up_weight[expert], preferred_element_type=jnp.float32)
        hidden = (jax.nn.silu(gate) * upper).astype(jnp.bfloat16)
        return jnp.dot(hidden, down_weight[expert], preferred_element_type=jnp.float32).astype(jnp.bfloat16)

    outputs = lax.map(one_expert, jnp.arange(EXPERTS, dtype=jnp.int32))
    weighted = pick_gates.reshape(-1)[:, None] * outputs.reshape(-1, D).astype(jnp.float32)
    branch = jnp.zeros((TOKENS, D), jnp.float32).at[pick_index.reshape(-1)].add(weighted)
    divisor = jnp.maximum(pick_counts, 1).astype(jnp.float32)
    return (rows.astype(jnp.float32) + branch / divisor[:, None]).astype(jnp.bfloat16)
```

```python
import jax
import jax.numpy as jnp
from jax import lax
from jax.sharding import PartitionSpec as P

BLOCK = 128
MOST = 3


def local(
    tokens, block_scales, pick_index, pick_gates, pick_counts, gate_weight, up_weight, down_weight
):
    tok_rows = tokens.shape[0]
    width = tokens.shape[1]
    n_wide = lax.axis_size("wide")
    n_narrow = lax.axis_size("narrow")
    my_rank = lax.axis_index("wide") * n_narrow + lax.axis_index("narrow")
    scaled = (
        tokens.astype(jnp.float32).reshape(tok_rows, width // BLOCK, BLOCK)
        * block_scales[:, :, None]
    )
    rows = scaled.reshape(tok_rows, width).astype(jnp.bfloat16)
    owners = pick_index // tok_rows
    mine = owners == my_rank
    order_in = jnp.cumsum(mine.astype(jnp.int32), axis=1) - 1
    slots = jnp.arange(MOST, dtype=jnp.int32)
    matched = mine[:, :, None] & (order_in[:, :, None] == slots[None, None, :])
    local_ids = pick_index - my_rank * tok_rows
    slot_token = jnp.sum(jnp.where(matched, local_ids[:, :, None], 0), axis=1)
    slot_valid = jnp.any(matched, axis=1)
    slot_gate = jnp.sum(jnp.where(matched, pick_gates[:, :, None], 0.0), axis=1)
    outgoing = rows[slot_token.reshape(-1)].reshape(n_wide, MOST, width)
    outgoing = jnp.where(slot_valid[:, :, None], outgoing, jnp.zeros_like(outgoing))
    arrived = lax.all_to_all(outgoing, "wide", split_axis=0, concat_axis=0, tiled=True)
    arrived = arrived.reshape(n_wide * MOST, width)
    flat_rows = lax.all_gather(arrived, "narrow", axis=0, tiled=True)
    gate = jnp.dot(flat_rows, gate_weight[0], preferred_element_type=jnp.float32)
    upper = jnp.dot(flat_rows, up_weight[0], preferred_element_type=jnp.float32)
    hidden = (jax.nn.silu(gate) * upper).astype(jnp.bfloat16)
    partial_out = jnp.dot(hidden, down_weight[0], preferred_element_type=jnp.float32)
    summed = lax.psum_scatter(partial_out, "narrow", scatter_dimension=0, tiled=True)
    summed = summed.astype(jnp.bfloat16).reshape(n_wide, MOST, width)
    expert_out = lax.all_to_all(summed, "wide", split_axis=0, concat_axis=0, tiled=True)
    token_ids = jnp.arange(tok_rows, dtype=jnp.int32)
    placing = (slot_token.reshape(-1)[:, None] == token_ids[None, :]) & slot_valid.reshape(-1)[
        :, None
    ]
    weights = jnp.where(placing, slot_gate.reshape(-1)[:, None], 0.0)
    branch = jnp.dot(
        weights.T,
        expert_out.reshape(-1, width).astype(jnp.float32),
        precision=lax.Precision.HIGHEST,
    )
    divisor = jnp.maximum(pick_counts, 1).astype(jnp.float32)
    return (rows.astype(jnp.float32) + branch / divisor[:, None]).astype(jnp.bfloat16)


def solution(mesh):
    return jax.shard_map(
        local,
        mesh=mesh,
        in_specs=(
            P(("wide", "narrow"), None),
            P(("wide", "narrow"), None),
            P(),
            P(),
            P(("wide", "narrow")),
            P("wide", None, "narrow"),
            P("wide", None, "narrow"),
            P("wide", "narrow", None),
        ),
        out_specs=P(("wide", "narrow"), None),
        check_vma=False,
    )
```

```python
import functools

import jax
import jax.numpy as jnp
from jax import lax
from jax.experimental import pallas as pl
from jax.experimental.pallas import tpu as pltpu
from jax.sharding import PartitionSpec as P

BLOCK = 128
MOST = 3
PIECE = 512
BF16 = jnp.bfloat16
F32 = jnp.float32
I32 = jnp.int32
MIB = 1024 * 1024


def mul(a, b):
    return jnp.dot(a, b, preferred_element_type=F32)


def mul_t(a, b):
    return lax.dot_general(a, b, (((1,), (1,)), ((), ())), preferred_element_type=F32)


def iota(shape, dim):
    return lax.broadcasted_iota(I32, shape, dim)


def third(q):
    return lax.shift_right_logical(q * 11, 5)


def slots_of(index, base, tok_rows, gates=None):
    cap = index.shape[1]
    local = index - base
    mine = (local >= 0) & (local < tok_rows)
    upper = (iota((cap, cap), 0) <= iota((cap, cap), 1)).astype(F32).astype(BF16)
    rank = mul(mine.astype(F32).astype(BF16), upper)
    hot = []
    for s in range(MOST):
        hit = mine & (rank == float(s + 1))
        token = jnp.sum(jnp.where(hit, local + 1, 0), axis=1, keepdims=True) - 1
        here = iota((index.shape[0], tok_rows), 1) == token
        value = 1.0
        if gates is not None:
            value = jnp.sum(jnp.where(hit, gates, 0.0), axis=1, keepdims=True)
        hot.append(jnp.where(here, value, 0.0))
    return jnp.concatenate(hot, axis=0)


def scale_columns(scales_ref, column_ref):
    scales = scales_ref[...]
    blank = jnp.zeros((BLOCK - scales.shape[0], scales.shape[1]), F32)
    column_ref[...] = jnp.transpose(jnp.concatenate([scales, blank], axis=0))


def scaled_piece(tokens, column, first):
    lane = iota(column.shape, 1)
    parts = []
    for b in range(tokens.shape[1] // BLOCK):
        part = tokens[:, b * BLOCK : (b + 1) * BLOCK].astype(F32)
        scale = jnp.sum(jnp.where(lane == first + b, column, 0.0), axis=1, keepdims=True)
        parts.append((part * scale).astype(BF16))
    return jnp.concatenate(parts, axis=1)


def put_piece(wide_ref, piece, experts, value):
    per = wide_ref.shape[1] // experts
    for s in range(MOST):
        at = pl.ds(piece * MOST + s, experts, stride=per)
        for q in range(PIECE // BLOCK):
            wide_ref[q, at, :] = value[
                s * experts : (s + 1) * experts, q * BLOCK : (q + 1) * BLOCK
            ]


def get_piece(wide_ref, piece, experts):
    per = wide_ref.shape[1] // experts
    lanes = []
    for q in range(PIECE // BLOCK):
        lanes.append(
            jnp.concatenate(
                [
                    wide_ref[q, pl.ds(piece * MOST + s, experts, stride=per), :]
                    for s in range(MOST)
                ],
                axis=0,
            )
        )
    return jnp.concatenate(lanes, axis=1).astype(BF16)


def narrow_raw(wide_ref, out_ref):
    for q in range(PIECE // BLOCK):
        out_ref[:, q * BLOCK : (q + 1) * BLOCK] = wide_ref[q].astype(BF16)


def widen_raw(raw_ref, wide_ref):
    for q in range(PIECE // BLOCK):
        wide_ref[q] = raw_ref[:, q * BLOCK : (q + 1) * BLOCK].astype(F32)


def dispatch_kernel(where_ref, index_ref, tokens_ref, scales_ref, out_ref, hot_ref, column_ref, raw_ref):
    step = pl.program_id(0)
    experts = index_ref.shape[0]
    tok_rows, chunk = tokens_ref.shape

    @pl.when(step == 0)
    def _():
        hot_ref[...] = slots_of(index_ref[...], where_ref[2], tok_rows).astype(BF16)
        scale_columns(scales_ref, column_ref)

    rows = scaled_piece(tokens_ref[...], column_ref[...], step * (chunk // BLOCK))
    picked = mul(hot_ref[...], rows)
    for k in range(chunk // PIECE):
        piece = step * (chunk // PIECE) + k
        put_piece(raw_ref, piece, experts, picked[:, k * PIECE : (k + 1) * PIECE])

    @pl.when(step == pl.num_programs(0) - 1)
    def _():
        narrow_raw(raw_ref, out_ref)


def here_mask(where_ref, index_ref, wide):
    mine = index_ref[pl.ds(where_ref[0], 1), :]
    tok_rows = where_ref[3]
    first = (iota((wide, mine.shape[1]), 0) * where_ref[4] + where_ref[1]) * tok_rows
    return ((mine >= first) & (mine < first + tok_rows)).astype(F32).astype(BF16)


def unpack_kernel(where_ref, index_ref, raw_ref, *refs):
    out_refs, wide_ref = refs[:-1], refs[-1]
    rows, half = out_refs[0].shape
    wide = index_ref.shape[0]
    widen_raw(raw_ref, wide_ref)
    for j in range(2 * half // PIECE):
        at = j * PIECE % half
        out_refs[j * PIECE // half][:, at : at + PIECE] = get_piece(wide_ref, j, wide)


def expert_kernel(blocks, steps, *refs):
    i = pl.program_id(0)
    xs, refs = refs[: 2 * blocks], refs[2 * blocks :]
    ws, downs, refs = refs[:8], refs[8:10], refs[10:]
    outs, accs = refs[: 2 * blocks], refs[2 * blocks :]
    left = jnp.concatenate([x[...] for x in xs[0::2]], axis=0)
    right = jnp.concatenate([x[...] for x in xs[1::2]], axis=0)

    @pl.when(i == 0)
    def _():
        for acc in accs:
            acc[...] = jnp.zeros_like(acc)

    for k, acc in enumerate(accs):
        acc[...] += mul_t(left, ws[2 * k][...]) + mul_t(right, ws[2 * k + 1][...])

    @pl.when(i == steps - 1)
    def _():
        hidden = []
        for gate, upper in ((accs[0], accs[1]), (accs[2], accs[3])):
            v = gate[...]
            hidden.append((v / (1.0 + jnp.exp(-v)) * upper[...]).astype(BF16))
        rows, half = outs[0].shape
        for c in range(2 * half // PIECE):
            cols = slice(c * PIECE, (c + 1) * PIECE)
            part = mul(hidden[0], downs[0][:, cols]) + mul(hidden[1], downs[1][:, cols])
            at = c * PIECE % half
            for b in range(blocks):
                out = outs[2 * b + c * PIECE // half]
                value = part[b * rows : (b + 1) * rows]
                out[:, at : at + PIECE] = value.astype(out.dtype)


def expert(xs, own, sibling, out_types):
    rows, half = xs[0][0].shape
    blocks = len(xs)
    hid = own[0].shape[0]
    width = 2 * half
    steps = 4
    deep = half // steps
    x_specs, w_specs, args, w_args = [], [], [], []
    for pair in xs:
        for x in pair:
            x_specs.append(pl.BlockSpec((rows, deep), lambda i: (0, i)))
            args.append(x)
    for w in (own[0], own[1], sibling[0], sibling[1]):
        w_specs.append(pl.BlockSpec((hid, deep), lambda i: (0, i)))
        w_specs.append(pl.BlockSpec((hid, deep), lambda i: (0, i + steps)))
        w_args += [w, w]
    d_specs = [pl.BlockSpec((hid, width), lambda i: (0, 0))] * 2
    return pl.pallas_call(
        functools.partial(expert_kernel, blocks, steps),
        grid=(steps,),
        in_specs=x_specs + w_specs + d_specs,
        out_specs=[pl.BlockSpec((rows, half), lambda i: (0, 0))] * (2 * blocks),
        out_shape=[jax.ShapeDtypeStruct((rows, half), t) for t in out_types],
        scratch_shapes=[pltpu.VMEM((rows * blocks, hid), F32)] * 4,
        compiler_params=pltpu.CompilerParams(vmem_limit_bytes=32 * MIB),
        cost_estimate=pl.CostEstimate(
            flops=2 * blocks * rows * hid * width * 6,
            bytes_accessed=hid * width * 12 + blocks * rows * width * 6,
            transcendentals=blocks * rows * hid * 2,
        ),
    )(*args, *w_args, own[2], sibling[2])


def pack_kernel(where_ref, index_ref, *refs):
    parts, out_ref, raw_ref = refs[:-2], refs[-2], refs[-1]
    rows, half = parts[0].shape
    wide = index_ref.shape[0]
    for j in range(2 * half // PIECE):
        at = j * PIECE % half
        summed = sum(p[:, at : at + PIECE].astype(F32) for p in parts[j * PIECE // half :: 2])
        put_piece(raw_ref, j, wide, summed)
    narrow_raw(raw_ref, out_ref)


def combine_kernel(
    where_ref, index_ref, gates_ref, counts_ref, tokens_ref, scales_ref, raw_ref, out_ref, weight_ref, column_ref, wide_ref
):
    step = pl.program_id(0)
    experts = index_ref.shape[0]
    tok_rows, chunk = tokens_ref.shape

    @pl.when(step == 0)
    def _():
        weight = slots_of(index_ref[...], where_ref[2], tok_rows, gates_ref[...])
        weight = weight / jnp.maximum(counts_ref[...], 1).astype(F32)
        high = weight.astype(BF16).astype(F32)
        both = jnp.concatenate([high, weight - high], axis=0)
        weight_ref[...] = jnp.transpose(both).astype(BF16)
        scale_columns(scales_ref, column_ref)
        widen_raw(raw_ref, wide_ref)

    pieces = chunk // PIECE
    got = [get_piece(wide_ref, step * pieces + k, experts) for k in range(pieces)]
    got = jnp.concatenate(got, axis=1)
    branch = mul(weight_ref[...], jnp.concatenate([got, got], axis=0))
    rows = scaled_piece(tokens_ref[...], column_ref[...], step * (chunk // BLOCK))
    out_ref[...] = (rows.astype(F32) + branch).astype(BF16)


def local(
    tokens, block_scales, pick_index, pick_gates, pick_counts, gate_weight, up_weight, down_weight
):
    tok_rows, width = tokens.shape
    n_wide = lax.axis_size("wide")
    n_narrow = lax.axis_size("narrow")
    at_wide = lax.axis_index("wide")
    at_narrow = lax.axis_index("narrow")
    other_core = [(i, i ^ 1) for i in range(n_narrow)]
    base = (at_wide * n_narrow + at_narrow) * tok_rows
    where = jnp.stack(
        [jnp.asarray(v, I32) for v in (at_wide, at_narrow, base, tok_rows, n_narrow)]
    )
    pieces = width // PIECE
    per = MOST * pieces
    total = n_wide * per
    scales = block_scales.T
    chunk = 2 * PIECE
    steps = width // chunk
    smem = pl.BlockSpec(memory_space=pltpu.SMEM)
    vmem = pl.BlockSpec(memory_space=pltpu.VMEM)

    def whole(a):
        return pl.BlockSpec(a.shape, lambda j: (0,) * a.ndim)

    def along_y(x, step):
        return lax.ppermute(
            x, "narrow", [(i, (i + 2 * step) % n_narrow) for i in range(n_narrow)]
        )

    own = (gate_weight[0].T, up_weight[0].T, down_weight[0])
    sibling = tuple(lax.ppermute(v, "narrow", other_core) for v in own)

    tokens_spec = pl.BlockSpec((tok_rows, chunk), lambda j: (0, j))
    column = pltpu.VMEM((tok_rows, BLOCK), F32)
    raw_f32 = pltpu.VMEM((PIECE // BLOCK, total, BLOCK), F32)
    raw_shape = jax.ShapeDtypeStruct((total, PIECE), BF16)
    outgoing = pl.pallas_call(
        dispatch_kernel,
        grid=(steps,),
        in_specs=[smem, whole(pick_index), tokens_spec, whole(scales)],
        out_specs=pl.BlockSpec((total, PIECE), lambda j: (0, 0)),
        out_shape=raw_shape,
        scratch_shapes=[pltpu.VMEM((MOST * n_wide, tok_rows), BF16), column, raw_f32],
        compiler_params=pltpu.CompilerParams(vmem_limit_bytes=56 * MIB),
    )(where, pick_index, tokens, scales)

    def exchange(raw):
        raw = raw.reshape(n_wide, per, PIECE)
        raw = lax.all_to_all(raw, "wide", split_axis=0, concat_axis=0, tiled=True)
        return raw.reshape(total, PIECE)

    arrived = exchange(outgoing)
    rows = n_wide * MOST
    half_shape = jax.ShapeDtypeStruct((rows, width // 2), BF16)
    x0 = pl.pallas_call(
        unpack_kernel,
        in_specs=[smem, vmem, vmem],
        out_specs=[vmem, vmem],
        out_shape=[half_shape, half_shape],
        scratch_shapes=[raw_f32],
        compiler_params=pltpu.CompilerParams(vmem_limit_bytes=24 * MIB),
    )(where, pick_index, arrived)

    xm = [None, None]
    xp = [None, None]
    xm[0] = along_y(x0[0], 1)
    xp[1] = along_y(x0[1], -1)
    xm[1] = along_y(x0[1], 1)
    xp[0] = along_y(x0[0], -1)
    x2 = (along_y(xm[0], 1), along_y(xp[1], -1))

    p0 = expert([x0], own, sibling, (F32, F32))
    pp_a, pp_b, pm_a, pm_b = expert([xp, xm], own, sibling, (F32, BF16, BF16, F32))
    p2 = expert([x2], own, sibling, (BF16, BF16))
    from_m = along_y(p2[0], 1)
    from_p = along_y(p2[1], -1)
    got_mb = along_y(pp_b, 1)
    got_pa = along_y(pm_a, -1)
    got_ma = along_y((pp_a + from_m.astype(F32)).astype(BF16), 1)
    got_pb = along_y((pm_b + from_p.astype(F32)).astype(BF16), -1)
    packed = pl.pallas_call(
        pack_kernel,
        in_specs=[smem] + [vmem] * 7,
        out_specs=vmem,
        out_shape=raw_shape,
        scratch_shapes=[raw_f32],
        compiler_params=pltpu.CompilerParams(vmem_limit_bytes=32 * MIB),
    )(where, pick_index, p0[0], p0[1], got_ma, got_mb, got_pa, got_pb)
    returned = exchange(packed)
    counts = pick_counts.reshape(1, tok_rows)
    return pl.pallas_call(
        combine_kernel,
        grid=(steps,),
        in_specs=[
            smem,
            whole(pick_index),
            whole(pick_gates),
            whole(counts),
            tokens_spec,
            whole(scales),
            whole(returned),
        ],
        out_specs=tokens_spec,
        out_shape=jax.ShapeDtypeStruct((tok_rows, width), BF16),
        scratch_shapes=[pltpu.VMEM((tok_rows, 2 * MOST * n_wide), BF16), column, raw_f32],
        compiler_params=pltpu.CompilerParams(vmem_limit_bytes=24 * MIB),
    )(where, pick_index, pick_gates, counts, tokens, scales, returned)


def solution(mesh):
    return jax.shard_map(
        local,
        mesh=mesh,
        in_specs=(
            P(("wide", "narrow"), None),
            P(("wide", "narrow"), None),
            P(),
            P(),
            P(("wide", "narrow")),
            P("wide", None, "narrow"),
            P("wide", None, "narrow"),
            P("wide", "narrow", None),
        ),
        out_specs=P(("wide", "narrow"), None),
        check_vma=False,
    )
```

```python
import functools

import jax
import jax.numpy as jnp
from jax import lax
from jax.experimental import pallas as pl
from jax.experimental.pallas import tpu as pltpu
from jax.sharding import PartitionSpec as P

BLOCK = 128
MOST = 3
PIECE = 512
BF16 = jnp.bfloat16
F32 = jnp.float32
I32 = jnp.int32
MIB = 1024 * 1024


def mul(a, b):
    return jnp.dot(a, b, preferred_element_type=F32)


def mul_t(a, b):
    return lax.dot_general(a, b, (((1,), (1,)), ((), ())), preferred_element_type=F32)


def iota(shape, dim):
    return lax.broadcasted_iota(I32, shape, dim)


def third(q):
    return lax.shift_right_logical(q * 11, 5)


def slots_of(index, base, tok_rows, gates=None):
    cap = index.shape[1]
    local = index - base
    mine = (local >= 0) & (local < tok_rows)
    upper = (iota((cap, cap), 0) <= iota((cap, cap), 1)).astype(F32).astype(BF16)
    rank = mul(mine.astype(F32).astype(BF16), upper)
    hot = []
    for s in range(MOST):
        hit = mine & (rank == float(s + 1))
        token = jnp.sum(jnp.where(hit, local + 1, 0), axis=1, keepdims=True) - 1
        here = iota((index.shape[0], tok_rows), 1) == token
        value = 1.0
        if gates is not None:
            value = jnp.sum(jnp.where(hit, gates, 0.0), axis=1, keepdims=True)
        hot.append(jnp.where(here, value, 0.0))
    return jnp.concatenate(hot, axis=0)


def scale_columns(scales_ref, column_ref):
    scales = scales_ref[...]
    blank = jnp.zeros((BLOCK - scales.shape[0], scales.shape[1]), F32)
    column_ref[...] = jnp.transpose(jnp.concatenate([scales, blank], axis=0))


def scaled_piece(tokens, column, first):
    lane = iota(column.shape, 1)
    parts = []
    for b in range(tokens.shape[1] // BLOCK):
        part = tokens[:, b * BLOCK : (b + 1) * BLOCK].astype(F32)
        scale = jnp.sum(jnp.where(lane == first + b, column, 0.0), axis=1, keepdims=True)
        parts.append((part * scale).astype(BF16))
    return jnp.concatenate(parts, axis=1)


def put_piece(wide_ref, piece, experts, value):
    per = wide_ref.shape[1] // experts
    for s in range(MOST):
        at = pl.ds(piece * MOST + s, experts, stride=per)
        for q in range(PIECE // BLOCK):
            wide_ref[q, at, :] = value[
                s * experts : (s + 1) * experts, q * BLOCK : (q + 1) * BLOCK
            ]


def get_piece(wide_ref, piece, experts):
    per = wide_ref.shape[1] // experts
    lanes = []
    for q in range(PIECE // BLOCK):
        lanes.append(
            jnp.concatenate(
                [
                    wide_ref[q, pl.ds(piece * MOST + s, experts, stride=per), :]
                    for s in range(MOST)
                ],
                axis=0,
            )
        )
    return jnp.concatenate(lanes, axis=1).astype(BF16)


def narrow_raw(wide_ref, out_ref):
    for q in range(PIECE // BLOCK):
        out_ref[:, q * BLOCK : (q + 1) * BLOCK] = wide_ref[q].astype(BF16)


def widen_raw(raw_ref, wide_ref):
    for q in range(PIECE // BLOCK):
        wide_ref[q] = raw_ref[:, q * BLOCK : (q + 1) * BLOCK].astype(F32)


def first_token(tok_rows):
    rank = lax.axis_index("wide") * lax.axis_size("narrow") + lax.axis_index("narrow")
    return rank * tok_rows


def most_rows(index, tok_rows, n_narrow):
    narrow = lax.shift_right_logical(index, tok_rows.bit_length() - 1) & (n_narrow - 1)
    most = jnp.zeros((index.shape[0], 1), F32)
    for n in range(n_narrow):
        held = jnp.sum(jnp.where(narrow == n, 1.0, 0.0), axis=1, keepdims=True)
        most = jnp.maximum(most, held)
    return jnp.max(most, axis=0, keepdims=True).astype(I32)


def dispatch_kernel(
    index_ref, tokens_ref, scales_ref, out_ref, most_ref, hot_ref, column_ref, raw_ref
):
    step = pl.program_id(0)
    experts = index_ref.shape[0]
    tok_rows, chunk = tokens_ref.shape

    @pl.when(step == 0)
    def _():
        hot_ref[...] = slots_of(index_ref[...], first_token(tok_rows), tok_rows).astype(BF16)
        scale_columns(scales_ref, column_ref)
        most_ref[...] = most_rows(index_ref[...], tok_rows, lax.axis_size("narrow"))

    rows = scaled_piece(tokens_ref[...], column_ref[...], step * (chunk // BLOCK))
    picked = mul(hot_ref[...], rows)
    for k in range(chunk // PIECE):
        piece = step * (chunk // PIECE) + k
        put_piece(raw_ref, piece, experts, picked[:, k * PIECE : (k + 1) * PIECE])

    @pl.when(step == pl.num_programs(0) - 1)
    def _():
        narrow_raw(raw_ref, out_ref)


def row_places(index_ref, tok_rows, first_row, rows):
    wide, cap = index_ref.shape
    n_narrow = lax.axis_size("narrow")
    mine = index_ref[pl.ds(lax.axis_index("wide"), 1), :]
    first = (iota((wide, cap), 0) * n_narrow + lax.axis_index("narrow")) * tok_rows
    inside = jnp.where((mine >= first) & (mine < first + tok_rows), 1.0, 0.0).astype(BF16)
    counts = mul_t(jnp.ones((8, cap), BF16), inside).astype(BF16)
    n = iota((wide, MOST * wide), 1)
    slot = (n >= wide).astype(I32) + (n >= 2 * wide).astype(I32)
    of, at = n - slot * wide, iota((wide, MOST * wide), 0)
    count = mul(counts, jnp.where(at == of, 1.0, 0.0).astype(BF16))[0:1]
    before = mul(counts, jnp.where(at < of, 1.0, 0.0).astype(BF16))[0:1]
    slot = slot[0:1].astype(F32)
    place = jnp.where(slot < count, before + slot, -1.0)
    hot = (iota((rows, MOST * wide), 0) + first_row).astype(F32) == place
    return jnp.where(hot, 1.0, 0.0).astype(BF16)


def unpack_kernel(tok_rows, first_row, index_ref, raw_ref, *refs):
    out_refs, wide_ref = refs[:-1], refs[-1]
    rows, half = out_refs[0].shape
    wide = index_ref.shape[0]
    widen_raw(raw_ref, wide_ref)
    places = row_places(index_ref, tok_rows, first_row, rows)
    for j in range(2 * half // PIECE):
        at = j * PIECE % half
        value = mul(places, get_piece(wide_ref, j, wide)).astype(BF16)
        out_refs[j * PIECE // half][:, at : at + PIECE] = value


def expert_kernel(blocks, *refs):
    xs, own, away, refs = (
        refs[: 2 * blocks],
        refs[2 * blocks : 2 * blocks + 2],
        refs[2 * blocks + 2 : 2 * blocks + 6],
        refs[2 * blocks + 6 :],
    )
    outs, held, sems = refs[: 2 * blocks], refs[2 * blocks : 2 * blocks + 4], refs[-1]
    copies = [pltpu.make_async_copy(away[k], held[k], sems.at[k]) for k in range(4)]
    for copy in copies:
        copy.start()
    left = jnp.concatenate([x[...] for x in xs[0::2]], axis=0)
    right = jnp.concatenate([x[...] for x in xs[1::2]], axis=0)
    rows, half = outs[0].shape
    hidden = []
    for gate_w, up_w in (own, held[:2]):
        if hidden:
            copies[0].wait()
            copies[1].wait()
        v = mul_t(gate_w[:, :half], left) + mul_t(gate_w[:, half:], right)
        u = mul_t(up_w[:, :half], left) + mul_t(up_w[:, half:], right)
        hidden.append(jnp.transpose(v / (1.0 + jnp.exp(-v)) * u).astype(BF16))
    copies[2].wait()
    copies[3].wait()
    for c in range(2 * half // PIECE):
        cols = slice(c * PIECE, (c + 1) * PIECE)
        part = mul(hidden[0], held[2][:, cols]) + mul(hidden[1], held[3][:, cols])
        at = c * PIECE % half
        for b in range(blocks):
            out = outs[2 * b + c * PIECE // half]
            out[:, at : at + PIECE] = part[b * rows : (b + 1) * rows].astype(out.dtype)


def expert(xs, own, sibling, out_types):
    rows, half = xs[0][0].shape
    blocks = len(xs)
    hid, width = own[2].shape
    args = [x for pair in xs for x in pair]
    away = [sibling[0], sibling[1], own[2], sibling[2]]
    args += [own[0], own[1], *away]
    vmem = pl.BlockSpec(memory_space=pltpu.VMEM)
    return pl.pallas_call(
        functools.partial(expert_kernel, blocks),
        in_specs=[vmem] * (len(args) - 4) + [pl.BlockSpec(memory_space=pl.ANY)] * 4,
        out_specs=[vmem] * (2 * blocks),
        out_shape=[jax.ShapeDtypeStruct((rows, half), t) for t in out_types],
        scratch_shapes=[pltpu.VMEM(w.shape, BF16) for w in away]
        + [pltpu.SemaphoreType.DMA((4,))],
        compiler_params=pltpu.CompilerParams(vmem_limit_bytes=30 * MIB),
        cost_estimate=pl.CostEstimate(flops=1, bytes_accessed=1, transcendentals=0),
    )(*args)


def pack_kernel(tok_rows, first_row, index_ref, *refs):
    parts, out_ref, raw_ref = refs[:6], refs[-2], refs[-1]
    rows, half = parts[0].shape
    wide = index_ref.shape[0]
    places = row_places(index_ref, tok_rows, first_row, rows)
    for j in range(2 * half // PIECE):
        at = j * PIECE % half
        summed = sum(p[:, at : at + PIECE].astype(F32) for p in parts[j * PIECE // half :: 2])
        summed = lax.dot_general(
            places,
            summed.astype(BF16),
            (((0,), (0,)), ((), ())),
            preferred_element_type=F32,
        )
        put_piece(raw_ref, j, wide, summed)
    narrow_raw(raw_ref, out_ref)
    if len(refs) > 8:
        out_ref[...] += refs[6][...]


def combine_kernel(
    index_ref, gates_ref, counts_ref, tokens_ref, scales_ref, raw_ref, out_ref, weight_ref, column_ref, wide_ref
):
    step = pl.program_id(0)
    experts = index_ref.shape[0]
    tok_rows, chunk = tokens_ref.shape

    @pl.when(step == 0)
    def _():
        weight = slots_of(index_ref[...], first_token(tok_rows), tok_rows, gates_ref[...])
        weight = weight / jnp.maximum(counts_ref[...], 1).astype(F32)
        high = weight.astype(BF16).astype(F32)
        both = jnp.concatenate([high, weight - high], axis=0)
        weight_ref[...] = jnp.transpose(both).astype(BF16)
        scale_columns(scales_ref, column_ref)
        widen_raw(raw_ref, wide_ref)

    pieces = chunk // PIECE
    got = [get_piece(wide_ref, step * pieces + k, experts) for k in range(pieces)]
    got = jnp.concatenate(got, axis=1)
    branch = mul(weight_ref[...], jnp.concatenate([got, got], axis=0))
    rows = scaled_piece(tokens_ref[...], column_ref[...], step * (chunk // BLOCK))
    out_ref[...] = (rows.astype(F32) + branch).astype(BF16)


def along_y(x, step):
    n = lax.axis_size("narrow")
    return lax.ppermute(x, "narrow", [(i, (i + 2 * step) % n) for i in range(n)])


def around_y(first_row, rows, tok_rows, arrived, pick_index, own, sibling, earlier=()):
    total = arrived.shape[0]
    width = own[2].shape[1]
    vmem = pl.BlockSpec(memory_space=pltpu.VMEM)
    raw_f32 = pltpu.VMEM((PIECE // BLOCK, total, BLOCK), F32)
    half_shape = jax.ShapeDtypeStruct((rows, width // 2), BF16)
    x0 = pl.pallas_call(
        functools.partial(unpack_kernel, tok_rows, first_row),
        in_specs=[vmem] * 2,
        out_specs=[vmem, vmem],
        out_shape=[half_shape, half_shape],
        scratch_shapes=[raw_f32],
        compiler_params=pltpu.CompilerParams(vmem_limit_bytes=24 * MIB),
    )(pick_index, arrived)

    xm, xp = [along_y(x0[0], 1), None], [None, along_y(x0[1], -1)]
    xm[1] = along_y(x0[1], 1)
    xp[0] = along_y(x0[0], -1)
    x2 = (along_y(xm[0], 1), along_y(xp[1], -1))

    p0 = expert([x0], own, sibling, (F32, F32))
    xp[0], xp[1], xm[0], xm[1] = lax.optimization_barrier((*xp, *xm, p0[0]))[:4]
    pp_a, pp_b, pm_a, pm_b = expert([xp, xm], own, sibling, (F32, BF16, BF16, F32))
    x2 = lax.optimization_barrier((*x2, pp_b))[:2]
    p2 = expert([x2], own, sibling, (BF16, BF16))
    got_mb = along_y(pp_b, 1)
    got_pa = along_y(pm_a, -1)
    from_m = along_y(p2[0], 1)
    from_p = along_y(p2[1], -1)
    from_m, got_mb = lax.optimization_barrier((from_m, got_mb))
    from_p, got_pa = lax.optimization_barrier((from_p, got_pa))
    got_ma = along_y((pp_a + from_m.astype(F32)).astype(BF16), 1)
    got_pb = along_y((pm_b + from_p.astype(F32)).astype(BF16), -1)
    return pl.pallas_call(
        functools.partial(pack_kernel, tok_rows, first_row),
        in_specs=[vmem] * (7 + len(earlier)),
        out_specs=vmem,
        out_shape=jax.ShapeDtypeStruct((total, PIECE), BF16),
        scratch_shapes=[raw_f32],
        compiler_params=pltpu.CompilerParams(vmem_limit_bytes=32 * MIB),
    )(pick_index, p0[0], p0[1], got_ma, got_mb, got_pa, got_pb, *earlier)


def local(
    tokens, block_scales, pick_index, pick_gates, pick_counts, gate_weight, up_weight, down_weight
):
    tok_rows, width = tokens.shape
    n_wide = lax.axis_size("wide")
    n_narrow = lax.axis_size("narrow")
    other_core = [(i, i ^ 1) for i in range(n_narrow)]
    pieces = width // PIECE
    per = MOST * pieces
    total = n_wide * per
    scales = block_scales.T
    chunk = 2 * PIECE
    steps = width // chunk

    def whole(a):
        return pl.BlockSpec(a.shape, lambda j: (0,) * a.ndim)

    own = (gate_weight[0].T, up_weight[0].T, down_weight[0])
    sibling = tuple(lax.ppermute(v, "narrow", other_core) for v in own)

    tokens_spec = pl.BlockSpec((tok_rows, chunk), lambda j: (0, j))
    column = pltpu.VMEM((tok_rows, BLOCK), F32)
    raw_f32 = pltpu.VMEM((PIECE // BLOCK, total, BLOCK), F32)
    raw_shape = jax.ShapeDtypeStruct((total, PIECE), BF16)
    outgoing, most = pl.pallas_call(
        dispatch_kernel,
        grid=(steps,),
        in_specs=[whole(pick_index), tokens_spec, whole(scales)],
        out_specs=[
            pl.BlockSpec((total, PIECE), lambda j: (0, 0)),
            pl.BlockSpec((1, 1), lambda j: (0, 0)),
        ],
        out_shape=[raw_shape, jax.ShapeDtypeStruct((1, 1), I32)],
        scratch_shapes=[pltpu.VMEM((MOST * n_wide, tok_rows), BF16), column, raw_f32],
        compiler_params=pltpu.CompilerParams(vmem_limit_bytes=56 * MIB),
    )(pick_index, tokens, scales)

    def exchange(raw):
        raw = raw.reshape(n_wide, per, PIECE)
        raw = lax.all_to_all(raw, "wide", split_axis=0, concat_axis=0, tiled=True)
        return raw.reshape(total, PIECE)

    arrived = exchange(outgoing)
    rows = MOST * n_wide * 3 // 4
    packed = around_y(0, rows, tok_rows, arrived, pick_index, own, sibling)

    def second(packed):
        return around_y(rows, rows // 2, tok_rows, arrived, pick_index, own, sibling, (packed,))

    packed = lax.cond(most[0, 0] > rows, second, lambda packed: packed, packed)
    returned = exchange(packed)
    counts = pick_counts.reshape(1, tok_rows)
    return pl.pallas_call(
        combine_kernel,
        grid=(steps,),
        in_specs=[
            whole(pick_index),
            whole(pick_gates),
            whole(counts),
            tokens_spec,
            whole(scales),
            whole(returned),
        ],
        out_specs=tokens_spec,
        out_shape=jax.ShapeDtypeStruct((tok_rows, width), BF16),
        scratch_shapes=[pltpu.VMEM((tok_rows, 2 * MOST * n_wide), BF16), column, raw_f32],
        compiler_params=pltpu.CompilerParams(vmem_limit_bytes=24 * MIB),
    )(pick_index, pick_gates, counts, tokens, scales, returned)


def solution(mesh):
    return jax.shard_map(
        local,
        mesh=mesh,
        in_specs=(
            P(("wide", "narrow"), None),
            P(("wide", "narrow"), None),
            P(),
            P(),
            P(("wide", "narrow")),
            P("wide", None, "narrow"),
            P("wide", None, "narrow"),
            P("wide", "narrow", None),
        ),
        out_specs=P(("wide", "narrow"), None),
        check_vma=False,
    )
```

```python
import functools

import jax
import jax.numpy as jnp
from jax import lax
from jax.experimental import pallas as pl
from jax.experimental.pallas import tpu as pltpu
from jax.sharding import PartitionSpec as P

BLOCK = 128
MOST = 3
PIECE = 512
BF16 = jnp.bfloat16
F32 = jnp.float32
I32 = jnp.int32
MIB = 1024 * 1024


def mul(a, b):
    return jnp.dot(a, b, preferred_element_type=F32)


def mul_t(a, b):
    return lax.dot_general(a, b, (((1,), (1,)), ((), ())), preferred_element_type=F32)


def iota(shape, dim):
    return lax.broadcasted_iota(I32, shape, dim)


def third(q):
    return lax.shift_right_logical(q * 11, 5)


def slots_of(index, base, tok_rows, gates=None):
    cap = index.shape[1]
    local = index - base
    mine = (local >= 0) & (local < tok_rows)
    upper = (iota((cap, cap), 0) <= iota((cap, cap), 1)).astype(F32).astype(BF16)
    rank = mul(mine.astype(F32).astype(BF16), upper)
    hot = []
    for s in range(MOST):
        hit = mine & (rank == float(s + 1))
        token = jnp.sum(jnp.where(hit, local + 1, 0), axis=1, keepdims=True) - 1
        here = iota((index.shape[0], tok_rows), 1) == token
        value = 1.0
        if gates is not None:
            value = jnp.sum(jnp.where(hit, gates, 0.0), axis=1, keepdims=True)
        hot.append(jnp.where(here, value, 0.0))
    return jnp.concatenate(hot, axis=0)


def scale_columns(rest):
    parts = []
    for _ in range(3):
        part = rest.astype(BF16).astype(F32)
        parts.append(part)
        rest = rest - part
    parts.append(jnp.zeros((BLOCK - 3 * rest.shape[0], rest.shape[1]), F32))
    return jnp.transpose(jnp.concatenate(parts, axis=0)).astype(BF16)


def scaled_piece(tokens, column, first, blocks):
    shape = (BLOCK, tokens.shape[1])
    lane = iota(shape, 0)
    third_of = (lane >= blocks).astype(I32) + (lane >= 2 * blocks).astype(I32)
    block = first + lax.shift_right_logical(iota(shape, 1), BLOCK.bit_length() - 1)
    spread = (lane - third_of * blocks == block) & (lane < 3 * blocks)
    scale = mul(column, jnp.where(spread, 1.0, 0.0).astype(BF16))
    return (tokens.astype(F32) * scale).astype(BF16)


def put_piece(wide_ref, piece, experts, value):
    per = wide_ref.shape[1] // experts
    for s in range(MOST):
        at = pl.ds(piece * MOST + s, experts, stride=per)
        for q in range(PIECE // BLOCK):
            wide_ref[q, at, :] = value[
                s * experts : (s + 1) * experts, q * BLOCK : (q + 1) * BLOCK
            ]


def get_piece(wide_ref, piece, experts):
    per = wide_ref.shape[1] // experts
    lanes = []
    for q in range(PIECE // BLOCK):
        lanes.append(
            jnp.concatenate(
                [
                    wide_ref[q, pl.ds(piece * MOST + s, experts, stride=per), :]
                    for s in range(MOST)
                ],
                axis=0,
            )
        )
    return jnp.concatenate(lanes, axis=1).astype(BF16)


def narrow_raw(wide_ref, out_ref):
    for q in range(PIECE // BLOCK):
        out_ref[:, q * BLOCK : (q + 1) * BLOCK] = wide_ref[q].astype(BF16)


def widen_raw(raw_ref, wide_ref):
    for q in range(PIECE // BLOCK):
        wide_ref[q] = raw_ref[:, q * BLOCK : (q + 1) * BLOCK].astype(F32)


def first_token(tok_rows):
    rank = lax.axis_index("wide") * lax.axis_size("narrow") + lax.axis_index("narrow")
    return rank * tok_rows


def most_rows(index, tok_rows, n_narrow):
    narrow = lax.shift_right_logical(index, tok_rows.bit_length() - 1) & (n_narrow - 1)
    most = jnp.zeros((index.shape[0], 1), F32)
    for n in range(n_narrow):
        held = jnp.sum(jnp.where(narrow == n, 1.0, 0.0), axis=1, keepdims=True)
        most = jnp.maximum(most, held)
    return jnp.max(most, axis=0, keepdims=True).astype(I32)


def dispatch_kernel(index_ref, scales_ref, tokens_ref, out_ref, most_ref, held_ref, raw_ref, sems):
    experts = index_ref.shape[0]
    chunks, tok_rows, chunk = held_ref.shape
    copies = []
    for k in range(chunks):
        part = tokens_ref.at[:, pl.ds(k * chunk, chunk)]
        copies.append(pltpu.make_async_copy(part, held_ref.at[k], sems.at[k]))
        copies[k].start()
    hot = slots_of(index_ref[...], first_token(tok_rows), tok_rows).astype(BF16)
    column = scale_columns(scales_ref[...])
    blocks = scales_ref.shape[0]
    most_ref[...] = most_rows(index_ref[...], tok_rows, lax.axis_size("narrow"))
    for k in range(chunks):
        copies[k].wait()
        picked = mul(hot, scaled_piece(held_ref[k], column, k * (chunk // BLOCK), blocks))
        for j in range(chunk // PIECE):
            piece = picked[:, j * PIECE : (j + 1) * PIECE]
            put_piece(raw_ref, k * (chunk // PIECE) + j, experts, piece)
    narrow_raw(raw_ref, out_ref)


def prepare_kernel(index_ref, gates_ref, counts_ref, scales_ref, tokens_ref, rows_ref, weight_ref):
    tok_rows, width = tokens_ref.shape
    weight = slots_of(index_ref[...], first_token(tok_rows), tok_rows, gates_ref[...])
    weight = weight / jnp.maximum(counts_ref[...], 1).astype(F32)
    high = weight.astype(BF16).astype(F32)
    both = jnp.concatenate([high, weight - high], axis=0)
    weight_ref[...] = jnp.transpose(both).astype(BF16)
    column = scale_columns(scales_ref[...])
    blocks = scales_ref.shape[0]
    for k in range(width // PIECE):
        cols = slice(k * PIECE, (k + 1) * PIECE)
        first = k * (PIECE // BLOCK)
        rows_ref[:, cols] = scaled_piece(tokens_ref[:, cols], column, first, blocks)


def row_places(index_ref, tok_rows, first_row, rows):
    wide, cap = index_ref.shape
    n_narrow = lax.axis_size("narrow")
    mine = index_ref[pl.ds(lax.axis_index("wide"), 1), :]
    first = (iota((wide, cap), 0) * n_narrow + lax.axis_index("narrow")) * tok_rows
    inside = jnp.where((mine >= first) & (mine < first + tok_rows), 1.0, 0.0).astype(BF16)
    counts = mul_t(jnp.ones((8, cap), BF16), inside).astype(BF16)
    n = iota((wide, MOST * wide), 1)
    slot = (n >= wide).astype(I32) + (n >= 2 * wide).astype(I32)
    of, at = n - slot * wide, iota((wide, MOST * wide), 0)
    count = mul(counts, jnp.where(at == of, 1.0, 0.0).astype(BF16))[0:1]
    before = mul(counts, jnp.where(at < of, 1.0, 0.0).astype(BF16))[0:1]
    slot = slot[0:1].astype(F32)
    place = jnp.where(slot < count, before + slot, -1.0)
    hot = (iota((rows, MOST * wide), 0) + first_row).astype(F32) == place
    return jnp.where(hot, 1.0, 0.0).astype(BF16)


def unpack_kernel(tok_rows, first_row, index_ref, raw_ref, *refs):
    out_refs, wide_ref = refs[:-1], refs[-1]
    rows, half = out_refs[0].shape
    wide = index_ref.shape[0]
    widen_raw(raw_ref, wide_ref)
    places = row_places(index_ref, tok_rows, first_row, rows)
    for j in range(2 * half // PIECE):
        at = j * PIECE % half
        value = mul(places, get_piece(wide_ref, j, wide)).astype(BF16)
        out_refs[j * PIECE // half][:, at : at + PIECE] = value


def expert_kernel(blocks, hold, *refs):
    xs, weights, outs = refs[: 2 * blocks], refs[2 * blocks : 2 * blocks + 6], refs[2 * blocks + 6 :]
    if hold:
        away, weights, sems = weights, outs[2 * blocks : -1], outs[-1]
        copies = [pltpu.make_async_copy(away[k], weights[k], sems.at[k]) for k in range(6)]
        for copy in copies:
            copy.start()
    left = jnp.concatenate([x[...] for x in xs[0::2]], axis=0)
    right = jnp.concatenate([x[...] for x in xs[1::2]], axis=0)
    rows, half = outs[0].shape
    hidden = []
    for k in (0, 2):
        gate_w, up_w = weights[k : k + 2]
        if hold:
            copies[k].wait()
            copies[k + 1].wait()
        v = mul_t(gate_w[:, :half], left) + mul_t(gate_w[:, half:], right)
        u = mul_t(up_w[:, :half], left) + mul_t(up_w[:, half:], right)
        hidden.append(jnp.transpose(v / (1.0 + jnp.exp(-v)) * u).astype(BF16))
    if hold:
        copies[4].wait()
        copies[5].wait()
    for c in range(2 * half // PIECE):
        cols = slice(c * PIECE, (c + 1) * PIECE)
        part = mul(hidden[0], weights[4][:, cols]) + mul(hidden[1], weights[5][:, cols])
        at = c * PIECE % half
        for b in range(blocks):
            out = outs[2 * b + c * PIECE // half]
            out[:, at : at + PIECE] = part[b * rows : (b + 1) * rows].astype(out.dtype)


def expert(xs, weights, out_types, hold=False):
    rows, half = xs[0][0].shape
    blocks = len(xs)
    args = [x for pair in xs for x in pair] + list(weights)
    vmem = pl.BlockSpec(memory_space=pltpu.VMEM)
    out_shape = [jax.ShapeDtypeStruct((rows, half), t) for t in out_types]
    scratch = []
    if hold:
        out_shape += [jax.ShapeDtypeStruct(w.shape, BF16) for w in weights]
        scratch = [pltpu.SemaphoreType.DMA((6,))]
    return pl.pallas_call(
        functools.partial(expert_kernel, blocks, hold),
        in_specs=[vmem] * (2 * blocks) + [pl.BlockSpec(memory_space=pl.ANY) if hold else vmem] * 6,
        out_specs=[vmem] * len(out_shape),
        out_shape=out_shape,
        scratch_shapes=scratch,
        compiler_params=pltpu.CompilerParams(vmem_limit_bytes=30 * MIB),
        cost_estimate=pl.CostEstimate(flops=1, bytes_accessed=1, transcendentals=0),
    )(*args)


def pack_kernel(tok_rows, index_ref, *refs):
    parts, late, out_ref, raw_ref = refs[:6], refs[6:8], refs[8], refs[9]
    rows, half = parts[0].shape
    wide = index_ref.shape[0]
    places = row_places(index_ref, tok_rows, 0, rows + late[0].shape[0])
    places = jnp.transpose(places.astype(F32)).astype(BF16)
    for j in range(2 * half // PIECE):
        side, at = j * PIECE // half, j * PIECE % half
        cols = slice(at, at + PIECE)
        summed = sum(p[:, cols].astype(F32) for p in parts[side::2])
        summed = jnp.concatenate([summed, late[side][:, cols].astype(F32)], axis=0)
        put_piece(raw_ref, j, wide, mul(places, summed.astype(BF16)))
    narrow_raw(raw_ref, out_ref)


def combine_kernel(weight_ref, raw_ref, rows_ref, out_ref, held_ref, wide_ref, sems):
    chunks, tok_rows, chunk = held_ref.shape
    experts = weight_ref.shape[1] // (2 * MOST)
    widen_raw(raw_ref, wide_ref)
    weight = weight_ref[...]
    copies = []
    for k in range(chunks):
        for j in range(chunk // PIECE):
            got = get_piece(wide_ref, k * (chunk // PIECE) + j, experts)
            branch = mul(weight, jnp.concatenate([got, got], axis=0))
            at = k * chunk + j * PIECE
            rows = rows_ref[:, at : at + PIECE].astype(F32)
            held_ref[k, :, j * PIECE : (j + 1) * PIECE] = (rows + branch).astype(BF16)
        part = out_ref.at[:, pl.ds(k * chunk, chunk)]
        copies.append(pltpu.make_async_copy(held_ref.at[k], part, sems.at[k]))
        copies[k].start()
    for copy in copies:
        copy.wait()


def along_y(x, step):
    n = lax.axis_size("narrow")
    return lax.ppermute(x, "narrow", [(i, (i + 2 * step) % n) for i in range(n)])


def around_y(first_row, rows, tok_rows, arrived, pick_index, own, sibling):
    total = arrived.shape[0]
    width = own[2].shape[1]
    vmem = pl.BlockSpec(memory_space=pltpu.VMEM)
    raw_f32 = pltpu.VMEM((PIECE // BLOCK, total, BLOCK), F32)
    half_shape = jax.ShapeDtypeStruct((rows, width // 2), BF16)
    x0 = pl.pallas_call(
        functools.partial(unpack_kernel, tok_rows, first_row),
        in_specs=[vmem] * 2,
        out_specs=[vmem, vmem],
        out_shape=[half_shape, half_shape],
        scratch_shapes=[raw_f32],
        compiler_params=pltpu.CompilerParams(vmem_limit_bytes=24 * MIB),
    )(pick_index, arrived)

    xm, xp = [along_y(x0[0], 1), None], [None, along_y(x0[1], -1)]
    xm[1] = along_y(x0[1], 1)
    xp[0] = along_y(x0[0], -1)
    x2 = (along_y(xm[0], 1), along_y(xp[1], -1))

    weights = (own[0], own[1], sibling[0], sibling[1], own[2], sibling[2])
    *p0, w0, w1, w2, w3, w4, w5 = expert([x0], weights, (F32, F32), hold=True)
    weights = (w0, w1, w2, w3, w4, w5)
    xp[0], xp[1], xm[0], xm[1] = lax.optimization_barrier((*xp, *xm, p0[0]))[:4]
    pp_a, pp_b, pm_a, pm_b = expert([xp, xm], weights, (F32, BF16, BF16, F32))
    x2 = lax.optimization_barrier((*x2, pp_b))[:2]
    p2 = expert([x2], weights, (BF16, BF16))
    got_mb = along_y(pp_b, 1)
    got_pa = along_y(pm_a, -1)
    from_m = along_y(p2[0], 1)
    from_p = along_y(p2[1], -1)
    from_m, got_mb, got_pa = lax.optimization_barrier((from_m, got_mb, got_pa))
    got_ma = along_y((pp_a + from_m.astype(F32)).astype(BF16), 1)
    got_pb = along_y((pm_b + from_p.astype(F32)).astype(BF16), -1)
    return p0[0], p0[1], got_ma, got_mb, got_pa, got_pb


def local(
    tokens, block_scales, pick_index, pick_gates, pick_counts, gate_weight, up_weight, down_weight
):
    tok_rows, width = tokens.shape
    n_wide = lax.axis_size("wide")
    n_narrow = lax.axis_size("narrow")
    other_core = [(i, i ^ 1) for i in range(n_narrow)]
    per = MOST * (width // PIECE)
    total = n_wide * per
    scales = block_scales.T
    chunk = 2 * PIECE
    chunks = width // chunk
    vmem = pl.BlockSpec(memory_space=pltpu.VMEM)
    anywhere = pl.BlockSpec(memory_space=pl.ANY)

    own = (gate_weight[0].T, up_weight[0].T, down_weight[0])
    sibling = tuple(lax.ppermute(v, "narrow", other_core) for v in own)

    raw_shape = jax.ShapeDtypeStruct((total, PIECE), BF16)
    raw_f32 = pltpu.VMEM((PIECE // BLOCK, total, BLOCK), F32)
    held = pltpu.VMEM((chunks, tok_rows, chunk), BF16)
    sems = pltpu.SemaphoreType.DMA((chunks,))
    outgoing, most = pl.pallas_call(
        dispatch_kernel,
        in_specs=[vmem, vmem, anywhere],
        out_specs=[vmem, vmem],
        out_shape=[raw_shape, jax.ShapeDtypeStruct((1, 1), I32)],
        scratch_shapes=[held, raw_f32, sems],
        compiler_params=pltpu.CompilerParams(vmem_limit_bytes=56 * MIB),
    )(pick_index, scales, tokens)

    def exchange(raw):
        raw = raw.reshape(n_wide, per, PIECE)
        raw = lax.all_to_all(raw, "wide", split_axis=0, concat_axis=0, tiled=True)
        return raw.reshape(total, PIECE)

    slots = MOST * n_wide
    rows_out, weight = pl.pallas_call(
        prepare_kernel,
        in_specs=[vmem] * 5,
        out_specs=[vmem] * 2,
        out_shape=[
            jax.ShapeDtypeStruct((tok_rows, width), BF16),
            jax.ShapeDtypeStruct((tok_rows, 2 * slots), BF16),
        ],
        compiler_params=pltpu.CompilerParams(vmem_limit_bytes=24 * MIB),
    )(pick_index, pick_gates, pick_counts.reshape(1, tok_rows), scales, tokens)

    arrived = exchange(outgoing)
    arrived, weight = lax.optimization_barrier((arrived, weight))
    rows = slots * 3 // 4
    parts = around_y(0, rows, tok_rows, arrived, pick_index, own, sibling)

    def second(arrived):
        late = around_y(rows, slots - rows, tok_rows, arrived, pick_index, own, sibling)
        return [sum(p.astype(F32) for p in late[side::2]).astype(BF16) for side in (0, 1)]

    def none(arrived):
        return [jnp.zeros((slots - rows, width // 2), BF16)] * 2

    arrived, *parts = lax.optimization_barrier((arrived, *parts))
    late = lax.cond(most[0, 0] > rows, second, none, arrived)
    packed = pl.pallas_call(
        functools.partial(pack_kernel, tok_rows),
        in_specs=[vmem] * 9,
        out_specs=vmem,
        out_shape=raw_shape,
        scratch_shapes=[raw_f32],
        compiler_params=pltpu.CompilerParams(vmem_limit_bytes=32 * MIB),
    )(pick_index, *parts, *late)
    returned = exchange(packed)
    return pl.pallas_call(
        combine_kernel,
        in_specs=[vmem] * 3,
        out_specs=anywhere,
        out_shape=jax.ShapeDtypeStruct((tok_rows, width), BF16),
        scratch_shapes=[held, raw_f32, sems],
        compiler_params=pltpu.CompilerParams(vmem_limit_bytes=24 * MIB),
    )(weight, returned, rows_out)


def solution(mesh):
    return jax.shard_map(
        local,
        mesh=mesh,
        in_specs=(
            P(("wide", "narrow"), None),
            P(("wide", "narrow"), None),
            P(),
            P(),
            P(("wide", "narrow")),
            P("wide", None, "narrow"),
            P("wide", None, "narrow"),
            P("wide", "narrow", None),
        ),
        out_specs=P(("wide", "narrow"), None),
        check_vma=False,
    )
```

```python
import functools

import jax
import jax.numpy as jnp
from jax import lax
from jax.experimental import pallas as pl
from jax.experimental.pallas import tpu as pltpu
from jax.sharding import PartitionSpec as P

BLOCK = 128
MOST = 3
PIECE = 512
BF16 = jnp.bfloat16
F32 = jnp.float32
I32 = jnp.int32
MIB = 1024 * 1024


def mul(a, b):
    return jnp.dot(a, b, preferred_element_type=F32)


def mul_t(a, b):
    return lax.dot_general(a, b, (((1,), (1,)), ((), ())), preferred_element_type=F32)


def iota(shape, dim):
    return lax.broadcasted_iota(I32, shape, dim)


def third(q):
    return lax.shift_right_logical(q * 11, 5)


def slots_of(index, base, tok_rows, gates=None):
    cap = index.shape[1]
    local = index - base
    mine = (local >= 0) & (local < tok_rows)
    upper = (iota((cap, cap), 0) <= iota((cap, cap), 1)).astype(F32).astype(BF16)
    rank = mul(mine.astype(F32).astype(BF16), upper)
    hot = []
    for s in range(MOST):
        hit = mine & (rank == float(s + 1))
        token = jnp.sum(jnp.where(hit, local + 1, 0), axis=1, keepdims=True) - 1
        here = iota((index.shape[0], tok_rows), 1) == token
        value = 1.0
        if gates is not None:
            value = jnp.sum(jnp.where(hit, gates, 0.0), axis=1, keepdims=True)
        hot.append(jnp.where(here, value, 0.0))
    return jnp.concatenate(hot, axis=0)


def scale_columns(rest):
    parts = []
    for _ in range(3):
        part = rest.astype(BF16).astype(F32)
        parts.append(part)
        rest = rest - part
    parts.append(jnp.zeros((BLOCK - 3 * rest.shape[0], rest.shape[1]), F32))
    return jnp.transpose(jnp.concatenate(parts, axis=0)).astype(BF16)


def scaled_piece(tokens, column, first, blocks):
    shape = (BLOCK, tokens.shape[1])
    lane = iota(shape, 0)
    third_of = (lane >= blocks).astype(I32) + (lane >= 2 * blocks).astype(I32)
    block = first + lax.shift_right_logical(iota(shape, 1), BLOCK.bit_length() - 1)
    spread = (lane - third_of * blocks == block) & (lane < 3 * blocks)
    scale = mul(column, jnp.where(spread, 1.0, 0.0).astype(BF16))
    return (tokens.astype(F32) * scale).astype(BF16)


def put_piece(wide_ref, piece, experts, value):
    per = wide_ref.shape[1] // experts
    for s in range(MOST):
        at = pl.ds(piece * MOST + s, experts, stride=per)
        for q in range(PIECE // BLOCK):
            wide_ref[q, at, :] = value[
                s * experts : (s + 1) * experts, q * BLOCK : (q + 1) * BLOCK
            ]


def get_piece(wide_ref, piece, experts):
    per = wide_ref.shape[1] // experts
    lanes = []
    for q in range(PIECE // BLOCK):
        lanes.append(
            jnp.concatenate(
                [
                    wide_ref[q, pl.ds(piece * MOST + s, experts, stride=per), :]
                    for s in range(MOST)
                ],
                axis=0,
            )
        )
    return jnp.concatenate(lanes, axis=1).astype(BF16)


def narrow_raw(wide_ref, out_ref):
    for q in range(PIECE // BLOCK):
        out_ref[:, q * BLOCK : (q + 1) * BLOCK] = wide_ref[q].astype(BF16)


def widen_raw(raw_ref, wide_ref):
    for q in range(PIECE // BLOCK):
        wide_ref[q] = raw_ref[:, q * BLOCK : (q + 1) * BLOCK].astype(F32)


def first_token(tok_rows):
    rank = lax.axis_index("wide") * lax.axis_size("narrow") + lax.axis_index("narrow")
    return rank * tok_rows


def most_rows(index, tok_rows, n_narrow):
    narrow = lax.shift_right_logical(index, tok_rows.bit_length() - 1) & (n_narrow - 1)
    most = jnp.zeros((index.shape[0], 1), F32)
    for n in range(n_narrow):
        held = jnp.sum(jnp.where(narrow == n, 1.0, 0.0), axis=1, keepdims=True)
        most = jnp.maximum(most, held)
    return jnp.max(most, axis=0, keepdims=True).astype(I32)


def dispatch_kernel(
    far_index, far_scales, tokens_ref, out_ref, most_ref, index_ref, scales_ref, held_ref, raw_ref, sems
):
    experts = index_ref.shape[0]
    chunks, tok_rows, chunk = held_ref.shape
    first = [
        pltpu.make_async_copy(far_index, index_ref, sems.at[chunks]),
        pltpu.make_async_copy(far_scales, scales_ref, sems.at[chunks + 1]),
    ]
    for copy in first:
        copy.start()
    copies = []
    for k in range(chunks):
        part = tokens_ref.at[:, pl.ds(k * chunk, chunk)]
        copies.append(pltpu.make_async_copy(part, held_ref.at[k], sems.at[k]))
        copies[k].start()
    for copy in first:
        copy.wait()
    hot = slots_of(index_ref[...], first_token(tok_rows), tok_rows).astype(BF16)
    column = scale_columns(scales_ref[...])
    blocks = scales_ref.shape[0]
    most_ref[...] = most_rows(index_ref[...], tok_rows, lax.axis_size("narrow"))
    for k in range(chunks):
        copies[k].wait()
        picked = mul(hot, scaled_piece(held_ref[k], column, k * (chunk // BLOCK), blocks))
        for j in range(chunk // PIECE):
            piece = picked[:, j * PIECE : (j + 1) * PIECE]
            put_piece(raw_ref, k * (chunk // PIECE) + j, experts, piece)
    narrow_raw(raw_ref, out_ref)


def prepare_kernel(index_ref, gates_ref, counts_ref, scales_ref, tokens_ref, rows_ref, weight_ref):
    tok_rows, width = tokens_ref.shape
    weight = slots_of(index_ref[...], first_token(tok_rows), tok_rows, gates_ref[...])
    weight = weight / jnp.maximum(counts_ref[...], 1).astype(F32)
    high = weight.astype(BF16).astype(F32)
    both = jnp.concatenate([high, weight - high], axis=0)
    weight_ref[...] = jnp.transpose(both).astype(BF16)
    column = scale_columns(scales_ref[...])
    blocks = scales_ref.shape[0]
    for k in range(width // PIECE):
        cols = slice(k * PIECE, (k + 1) * PIECE)
        first = k * (PIECE // BLOCK)
        rows_ref[:, cols] = scaled_piece(tokens_ref[:, cols], column, first, blocks)


def row_places(index_ref, tok_rows, first_row, rows):
    wide, cap = index_ref.shape
    n_narrow = lax.axis_size("narrow")
    mine = index_ref[pl.ds(lax.axis_index("wide"), 1), :]
    first = (iota((wide, cap), 0) * n_narrow + lax.axis_index("narrow")) * tok_rows
    inside = jnp.where((mine >= first) & (mine < first + tok_rows), 1.0, 0.0).astype(BF16)
    counts = mul_t(jnp.ones((8, cap), BF16), inside).astype(BF16)
    n = iota((wide, MOST * wide), 1)
    slot = (n >= wide).astype(I32) + (n >= 2 * wide).astype(I32)
    of, at = n - slot * wide, iota((wide, MOST * wide), 0)
    count = mul(counts, jnp.where(at == of, 1.0, 0.0).astype(BF16))[0:1]
    before = mul(counts, jnp.where(at < of, 1.0, 0.0).astype(BF16))[0:1]
    slot = slot[0:1].astype(F32)
    place = jnp.where(slot < count, before + slot, -1.0)
    hot = (iota((rows, MOST * wide), 0) + first_row).astype(F32) == place
    return jnp.where(hot, 1.0, 0.0).astype(BF16)


def unpack_kernel(tok_rows, first_row, index_ref, raw_ref, *refs):
    out_refs, wide_ref = refs[:-1], refs[-1]
    rows, half = out_refs[0].shape
    wide = index_ref.shape[0]
    widen_raw(raw_ref, wide_ref)
    places = row_places(index_ref, tok_rows, first_row, rows)
    for j in range(2 * half // PIECE):
        at = j * PIECE % half
        value = mul(places, get_piece(wide_ref, j, wide)).astype(BF16)
        out_refs[j * PIECE // half][:, at : at + PIECE] = value


def expert_kernel(blocks, hold, *refs):
    xs, weights, outs = refs[: 2 * blocks], refs[2 * blocks : 2 * blocks + 6], refs[2 * blocks + 6 :]
    if hold:
        away, weights, sems = weights, outs[2 * blocks : -1], outs[-1]
        copies = [pltpu.make_async_copy(away[k], weights[k], sems.at[k]) for k in range(6)]
        for copy in copies:
            copy.start()
    left = jnp.concatenate([x[...] for x in xs[0::2]], axis=0)
    right = jnp.concatenate([x[...] for x in xs[1::2]], axis=0)
    rows, half = outs[0].shape
    hidden = []
    for k in (0, 2):
        gate_w, up_w = weights[k : k + 2]
        if hold:
            copies[k].wait()
            copies[k + 1].wait()
        v = mul_t(gate_w[:, :half], left) + mul_t(gate_w[:, half:], right)
        u = mul_t(up_w[:, :half], left) + mul_t(up_w[:, half:], right)
        hidden.append(jnp.transpose(v / (1.0 + jnp.exp(-v)) * u).astype(BF16))
    if hold:
        copies[4].wait()
        copies[5].wait()
    for c in range(2 * half // PIECE):
        cols = slice(c * PIECE, (c + 1) * PIECE)
        part = mul(hidden[0], weights[4][:, cols]) + mul(hidden[1], weights[5][:, cols])
        at = c * PIECE % half
        for b in range(blocks):
            out = outs[2 * b + c * PIECE // half]
            out[:, at : at + PIECE] = part[b * rows : (b + 1) * rows].astype(out.dtype)


def expert(xs, weights, out_types, hold=False):
    rows, half = xs[0][0].shape
    blocks = len(xs)
    args = [x for pair in xs for x in pair] + list(weights)
    vmem = pl.BlockSpec(memory_space=pltpu.VMEM)
    out_shape = [jax.ShapeDtypeStruct((rows, half), t) for t in out_types]
    scratch = []
    if hold:
        out_shape += [jax.ShapeDtypeStruct(w.shape, BF16) for w in weights]
        scratch = [pltpu.SemaphoreType.DMA((6,))]
    return pl.pallas_call(
        functools.partial(expert_kernel, blocks, hold),
        in_specs=[vmem] * (2 * blocks) + [pl.BlockSpec(memory_space=pl.ANY) if hold else vmem] * 6,
        out_specs=[vmem] * len(out_shape),
        out_shape=out_shape,
        scratch_shapes=scratch,
        compiler_params=pltpu.CompilerParams(vmem_limit_bytes=30 * MIB),
        cost_estimate=pl.CostEstimate(flops=1, bytes_accessed=1, transcendentals=0),
    )(*args)


def pack_kernel(tok_rows, index_ref, *refs):
    parts, late, out_ref, raw_ref = refs[:6], refs[6:8], refs[8], refs[9]
    rows, half = parts[0].shape
    wide = index_ref.shape[0]
    places = row_places(index_ref, tok_rows, 0, rows + late[0].shape[0])
    places = jnp.transpose(places.astype(F32)).astype(BF16)
    for j in range(2 * half // PIECE):
        side, at = j * PIECE // half, j * PIECE % half
        cols = slice(at, at + PIECE)
        summed = sum(p[:, cols].astype(F32) for p in parts[side::2])
        summed = jnp.concatenate([summed, late[side][:, cols].astype(F32)], axis=0)
        put_piece(raw_ref, j, wide, mul(places, summed.astype(BF16)))
    narrow_raw(raw_ref, out_ref)


def combine_kernel(weight_ref, raw_ref, rows_ref, out_ref, held_ref, wide_ref, sems):
    chunks, tok_rows, chunk = held_ref.shape
    experts = weight_ref.shape[1] // (2 * MOST)
    widen_raw(raw_ref, wide_ref)
    weight = weight_ref[...]
    copies = []
    for k in range(chunks):
        for j in range(chunk // PIECE):
            got = get_piece(wide_ref, k * (chunk // PIECE) + j, experts)
            branch = mul(weight, jnp.concatenate([got, got], axis=0))
            at = k * chunk + j * PIECE
            rows = rows_ref[:, at : at + PIECE].astype(F32)
            held_ref[k, :, j * PIECE : (j + 1) * PIECE] = (rows + branch).astype(BF16)
        part = out_ref.at[:, pl.ds(k * chunk, chunk)]
        copies.append(pltpu.make_async_copy(held_ref.at[k], part, sems.at[k]))
        copies[k].start()
    for copy in copies:
        copy.wait()


def along_y(x, step):
    n = lax.axis_size("narrow")
    return lax.ppermute(x, "narrow", [(i, (i + 2 * step) % n) for i in range(n)])


def around_y(first_row, rows, tok_rows, arrived, pick_index, own, sibling):
    total = arrived.shape[0]
    width = own[2].shape[1]
    vmem = pl.BlockSpec(memory_space=pltpu.VMEM)
    raw_f32 = pltpu.VMEM((PIECE // BLOCK, total, BLOCK), F32)
    half_shape = jax.ShapeDtypeStruct((rows, width // 2), BF16)
    x0 = pl.pallas_call(
        functools.partial(unpack_kernel, tok_rows, first_row),
        in_specs=[vmem] * 2,
        out_specs=[vmem, vmem],
        out_shape=[half_shape, half_shape],
        scratch_shapes=[raw_f32],
        compiler_params=pltpu.CompilerParams(vmem_limit_bytes=24 * MIB),
    )(pick_index, arrived)

    xm, xp = [along_y(x0[0], 1), None], [None, along_y(x0[1], -1)]
    xm[1] = along_y(x0[1], 1)
    xp[0] = along_y(x0[0], -1)
    x2 = (along_y(xm[0], 1), along_y(xp[1], -1))

    weights = (own[0], own[1], sibling[0], sibling[1], own[2], sibling[2])
    *p0, w0, w1, w2, w3, w4, w5 = expert([x0], weights, (F32, F32), hold=True)
    weights = (w0, w1, w2, w3, w4, w5)
    xp[0], xp[1], xm[0], xm[1] = lax.optimization_barrier((*xp, *xm, p0[0]))[:4]
    pp_a, pp_b, pm_a, pm_b = expert([xp, xm], weights, (F32, BF16, BF16, F32))
    x2 = lax.optimization_barrier((*x2, pp_b))[:2]
    p2 = expert([x2], weights, (BF16, BF16))
    got_mb = along_y(pp_b, 1)
    got_pa = along_y(pm_a, -1)
    from_m = along_y(p2[0], 1)
    from_p = along_y(p2[1], -1)
    from_m, got_mb, got_pa = lax.optimization_barrier((from_m, got_mb, got_pa))
    got_ma = along_y((pp_a + from_m.astype(F32)).astype(BF16), 1)
    got_pb = along_y((pm_b + from_p.astype(F32)).astype(BF16), -1)
    return p0[0], p0[1], got_ma, got_mb, got_pa, got_pb


def local(
    tokens, block_scales, pick_index, pick_gates, pick_counts, gate_weight, up_weight, down_weight
):
    tok_rows, width = tokens.shape
    n_wide = lax.axis_size("wide")
    n_narrow = lax.axis_size("narrow")
    other_core = [(i, i ^ 1) for i in range(n_narrow)]
    per = MOST * (width // PIECE)
    total = n_wide * per
    scales = block_scales.T
    chunk = 2 * PIECE
    chunks = width // chunk
    vmem = pl.BlockSpec(memory_space=pltpu.VMEM)
    anywhere = pl.BlockSpec(memory_space=pl.ANY)

    own = (gate_weight[0].T, up_weight[0].T, down_weight[0])
    sibling = tuple(lax.ppermute(v, "narrow", other_core) for v in own)

    raw_shape = jax.ShapeDtypeStruct((total, PIECE), BF16)
    raw_f32 = pltpu.VMEM((PIECE // BLOCK, total, BLOCK), F32)
    held = pltpu.VMEM((chunks, tok_rows, chunk), BF16)
    sems = pltpu.SemaphoreType.DMA((chunks,))
    outgoing, most = pl.pallas_call(
        dispatch_kernel,
        in_specs=[anywhere] * 3,
        out_specs=[vmem, vmem],
        out_shape=[raw_shape, jax.ShapeDtypeStruct((1, 1), I32)],
        scratch_shapes=[
            pltpu.VMEM(pick_index.shape, I32),
            pltpu.VMEM(scales.shape, F32),
            held,
            raw_f32,
            pltpu.SemaphoreType.DMA((chunks + 2,)),
        ],
        compiler_params=pltpu.CompilerParams(vmem_limit_bytes=56 * MIB),
    )(pick_index, scales, tokens)

    def exchange(raw):
        raw = raw.reshape(n_wide, per, PIECE)
        raw = lax.all_to_all(raw, "wide", split_axis=0, concat_axis=0, tiled=True)
        return raw.reshape(total, PIECE)

    slots = MOST * n_wide
    rows_out, weight = pl.pallas_call(
        prepare_kernel,
        in_specs=[vmem] * 5,
        out_specs=[vmem] * 2,
        out_shape=[
            jax.ShapeDtypeStruct((tok_rows, width), BF16),
            jax.ShapeDtypeStruct((tok_rows, 2 * slots), BF16),
        ],
        compiler_params=pltpu.CompilerParams(vmem_limit_bytes=24 * MIB),
    )(pick_index, pick_gates, pick_counts.reshape(1, tok_rows), scales, tokens)

    arrived = exchange(outgoing)
    arrived, weight = lax.optimization_barrier((arrived, weight))
    rows = slots * 3 // 4
    parts = around_y(0, rows, tok_rows, arrived, pick_index, own, sibling)

    def second(arrived):
        late = around_y(rows, slots - rows, tok_rows, arrived, pick_index, own, sibling)
        return [sum(p.astype(F32) for p in late[side::2]).astype(BF16) for side in (0, 1)]

    def none(arrived):
        return [jnp.zeros((slots - rows, width // 2), BF16)] * 2

    arrived, *parts = lax.optimization_barrier((arrived, *parts))
    late = lax.cond(most[0, 0] > rows, second, none, arrived)
    packed = pl.pallas_call(
        functools.partial(pack_kernel, tok_rows),
        in_specs=[vmem] * 9,
        out_specs=vmem,
        out_shape=raw_shape,
        scratch_shapes=[raw_f32],
        compiler_params=pltpu.CompilerParams(vmem_limit_bytes=32 * MIB),
    )(pick_index, *parts, *late)
    returned = exchange(packed)
    return pl.pallas_call(
        combine_kernel,
        in_specs=[vmem] * 3,
        out_specs=anywhere,
        out_shape=jax.ShapeDtypeStruct((tok_rows, width), BF16),
        scratch_shapes=[held, raw_f32, sems],
        compiler_params=pltpu.CompilerParams(vmem_limit_bytes=24 * MIB),
    )(weight, returned, rows_out)


def solution(mesh):
    return jax.shard_map(
        local,
        mesh=mesh,
        in_specs=(
            P(("wide", "narrow"), None),
            P(("wide", "narrow"), None),
            P(),
            P(),
            P(("wide", "narrow")),
            P("wide", None, "narrow"),
            P("wide", None, "narrow"),
            P("wide", "narrow", None),
        ),
        out_specs=P(("wide", "narrow"), None),
        check_vma=False,
    )
```

```python
import functools

import jax
import jax.numpy as jnp
from jax import lax
from jax.experimental import pallas as pl
from jax.experimental.pallas import tpu as pltpu
from jax.sharding import PartitionSpec as P

BLOCK = 128
MOST = 3
PIECE = 512
BF16 = jnp.bfloat16
F32 = jnp.float32
I32 = jnp.int32
MIB = 1024 * 1024


def mul(a, b):
    return jnp.dot(a, b, preferred_element_type=F32)


def mul_t(a, b):
    return lax.dot_general(a, b, (((1,), (1,)), ((), ())), preferred_element_type=F32)


def iota(shape, dim):
    return lax.broadcasted_iota(I32, shape, dim)


def third(q):
    return lax.shift_right_logical(q * 11, 5)


def slots_of(index, base, tok_rows, gates=None):
    cap = index.shape[1]
    local = index - base
    mine = (local >= 0) & (local < tok_rows)
    upper = (iota((cap, cap), 0) <= iota((cap, cap), 1)).astype(F32).astype(BF16)
    rank = mul(mine.astype(F32).astype(BF16), upper)
    hot = []
    for s in range(MOST):
        hit = mine & (rank == float(s + 1))
        token = jnp.sum(jnp.where(hit, local + 1, 0), axis=1, keepdims=True) - 1
        here = iota((index.shape[0], tok_rows), 1) == token
        value = 1.0
        if gates is not None:
            value = jnp.sum(jnp.where(hit, gates, 0.0), axis=1, keepdims=True)
        hot.append(jnp.where(here, value, 0.0))
    return jnp.concatenate(hot, axis=0)


def scale_columns(rest):
    parts = []
    for _ in range(3):
        part = rest.astype(BF16).astype(F32)
        parts.append(part)
        rest = rest - part
    parts.append(jnp.zeros((BLOCK - 3 * rest.shape[0], rest.shape[1]), F32))
    return jnp.transpose(jnp.concatenate(parts, axis=0)).astype(BF16)


def scaled_piece(tokens, column, first, blocks):
    shape = (BLOCK, tokens.shape[1])
    lane = iota(shape, 0)
    third_of = (lane >= blocks).astype(I32) + (lane >= 2 * blocks).astype(I32)
    block = first + lax.shift_right_logical(iota(shape, 1), BLOCK.bit_length() - 1)
    spread = (lane - third_of * blocks == block) & (lane < 3 * blocks)
    scale = mul(column, jnp.where(spread, 1.0, 0.0).astype(BF16))
    return (tokens.astype(F32) * scale).astype(BF16)


def put_piece(wide_ref, piece, experts, value):
    per = wide_ref.shape[1] // experts
    for s in range(MOST):
        at = pl.ds(piece * MOST + s, experts, stride=per)
        for q in range(PIECE // BLOCK):
            wide_ref[q, at, :] = value[
                s * experts : (s + 1) * experts, q * BLOCK : (q + 1) * BLOCK
            ]


def get_piece(wide_ref, piece, experts):
    per = wide_ref.shape[1] // experts
    lanes = []
    for q in range(PIECE // BLOCK):
        lanes.append(
            jnp.concatenate(
                [
                    wide_ref[q, pl.ds(piece * MOST + s, experts, stride=per), :]
                    for s in range(MOST)
                ],
                axis=0,
            )
        )
    return jnp.concatenate(lanes, axis=1).astype(BF16)


def narrow_raw(wide_ref, out_ref):
    total = out_ref.shape[0]
    for q in range(PIECE // BLOCK):
        out_ref[:, q * BLOCK : (q + 1) * BLOCK] = wide_ref[q, :total, :].astype(BF16)


def widen_raw(raw_ref, wide_ref):
    for q in range(PIECE // BLOCK):
        part = raw_ref[:, q * BLOCK : (q + 1) * BLOCK].astype(F32)
        wide_ref[q, : raw_ref.shape[0], :] = part


def first_token(tok_rows):
    rank = lax.axis_index("wide") * lax.axis_size("narrow") + lax.axis_index("narrow")
    return rank * tok_rows


def most_rows(index, tok_rows, n_narrow):
    narrow = lax.shift_right_logical(index, tok_rows.bit_length() - 1) & (n_narrow - 1)
    most = jnp.zeros((index.shape[0], 1), F32)
    for n in range(n_narrow):
        held = jnp.sum(jnp.where(narrow == n, 1.0, 0.0), axis=1, keepdims=True)
        most = jnp.maximum(most, held)
    return jnp.max(most, axis=0, keepdims=True).astype(I32)


def dispatch_kernel(
    far_index, far_scales, tokens_ref, out_ref, most_ref, index_ref, scales_ref, held_ref, raw_ref, sems
):
    experts = index_ref.shape[0]
    chunks, tok_rows, chunk = held_ref.shape
    first = [
        pltpu.make_async_copy(far_index, index_ref, sems.at[chunks]),
        pltpu.make_async_copy(far_scales, scales_ref, sems.at[chunks + 1]),
    ]
    for copy in first:
        copy.start()
    copies = []
    for k in range(chunks):
        part = tokens_ref.at[:, pl.ds(k * chunk, chunk)]
        copies.append(pltpu.make_async_copy(part, held_ref.at[k], sems.at[k]))
        copies[k].start()
    for copy in first:
        copy.wait()
    hot = slots_of(index_ref[...], first_token(tok_rows), tok_rows).astype(BF16)
    column = scale_columns(scales_ref[...])
    blocks = scales_ref.shape[0]
    most_ref[...] = most_rows(index_ref[...], tok_rows, lax.axis_size("narrow"))
    for k in range(chunks):
        copies[k].wait()
        picked = mul(hot, scaled_piece(held_ref[k], column, k * (chunk // BLOCK), blocks))
        for j in range(chunk // PIECE):
            piece = picked[:, j * PIECE : (j + 1) * PIECE]
            put_piece(raw_ref, k * (chunk // PIECE) + j, experts, piece)
    narrow_raw(raw_ref, out_ref)


def prepare_kernel(index_ref, gates_ref, counts_ref, scales_ref, tokens_ref, rows_ref, weight_ref):
    tok_rows, width = tokens_ref.shape
    weight = slots_of(index_ref[...], first_token(tok_rows), tok_rows, gates_ref[...])
    weight = weight / jnp.maximum(counts_ref[...], 1).astype(F32)
    high = weight.astype(BF16).astype(F32)
    both = jnp.concatenate([high, weight - high], axis=0)
    weight_ref[...] = jnp.transpose(both).astype(BF16)
    column = scale_columns(scales_ref[...])
    blocks = scales_ref.shape[0]
    for k in range(width // PIECE):
        cols = slice(k * PIECE, (k + 1) * PIECE)
        first = k * (PIECE // BLOCK)
        rows_ref[:, cols] = scaled_piece(tokens_ref[:, cols], column, first, blocks)


def row_places(index_ref, tok_rows, first_row, rows):
    wide, cap = index_ref.shape
    n_narrow = lax.axis_size("narrow")
    mine = index_ref[pl.ds(lax.axis_index("wide"), 1), :]
    first = (iota((wide, cap), 0) * n_narrow + lax.axis_index("narrow")) * tok_rows
    inside = jnp.where((mine >= first) & (mine < first + tok_rows), 1.0, 0.0).astype(BF16)
    counts = mul_t(jnp.ones((8, cap), BF16), inside).astype(BF16)
    n = iota((wide, MOST * wide), 1)
    slot = (n >= wide).astype(I32) + (n >= 2 * wide).astype(I32)
    of, at = n - slot * wide, iota((wide, MOST * wide), 0)
    count = mul(counts, jnp.where(at == of, 1.0, 0.0).astype(BF16))[0:1]
    before = mul(counts, jnp.where(at < of, 1.0, 0.0).astype(BF16))[0:1]
    slot = slot[0:1].astype(F32)
    place = jnp.where(slot < count, before + slot, -1.0)
    hot = (iota((rows, MOST * wide), 0) + first_row).astype(F32) == place
    return jnp.where(hot, 1.0, 0.0).astype(BF16)


def unpack_kernel(tok_rows, first_row, index_ref, raw_ref, *refs):
    out_refs, wide_ref = refs[:-1], refs[-1]
    rows, half = out_refs[0].shape
    wide = index_ref.shape[0]
    widen_raw(raw_ref, wide_ref)
    places = row_places(index_ref, tok_rows, first_row, rows)
    for j in range(2 * half // PIECE):
        at = j * PIECE % half
        value = mul(places, get_piece(wide_ref, j, wide)).astype(BF16)
        out_refs[j * PIECE // half][:, at : at + PIECE] = value


def expert_kernel(blocks, hold, *refs):
    xs, weights, outs = refs[: 2 * blocks], refs[2 * blocks : 2 * blocks + 6], refs[2 * blocks + 6 :]
    if hold:
        away, weights, sems = weights, outs[2 * blocks : -1], outs[-1]
        copies = [pltpu.make_async_copy(away[k], weights[k], sems.at[k]) for k in range(6)]
        for copy in copies:
            copy.start()
    left = jnp.concatenate([x[...] for x in xs[0::2]], axis=0)
    right = jnp.concatenate([x[...] for x in xs[1::2]], axis=0)
    rows, half = outs[0].shape
    hidden = []
    for k in (0, 2):
        gate_w, up_w = weights[k : k + 2]
        if hold:
            copies[k].wait()
            copies[k + 1].wait()
        v = mul_t(gate_w[:, :half], left) + mul_t(gate_w[:, half:], right)
        u = mul_t(up_w[:, :half], left) + mul_t(up_w[:, half:], right)
        hidden.append(jnp.transpose(v / (1.0 + jnp.exp(-v)) * u).astype(BF16))
    if hold:
        copies[4].wait()
        copies[5].wait()
    for c in range(2 * half // PIECE):
        cols = slice(c * PIECE, (c + 1) * PIECE)
        part = mul(hidden[0], weights[4][:, cols]) + mul(hidden[1], weights[5][:, cols])
        at = c * PIECE % half
        for b in range(blocks):
            out = outs[2 * b + c * PIECE // half]
            out[:, at : at + PIECE] = part[b * rows : (b + 1) * rows].astype(out.dtype)


def expert(xs, weights, out_types, hold=False):
    rows, half = xs[0][0].shape
    blocks = len(xs)
    args = [x for pair in xs for x in pair] + list(weights)
    vmem = pl.BlockSpec(memory_space=pltpu.VMEM)
    out_shape = [jax.ShapeDtypeStruct((rows, half), t) for t in out_types]
    scratch = []
    if hold:
        out_shape += [jax.ShapeDtypeStruct(w.shape, BF16) for w in weights]
        scratch = [pltpu.SemaphoreType.DMA((6,))]
    return pl.pallas_call(
        functools.partial(expert_kernel, blocks, hold),
        in_specs=[vmem] * (2 * blocks) + [pl.BlockSpec(memory_space=pl.ANY) if hold else vmem] * 6,
        out_specs=[vmem] * len(out_shape),
        out_shape=out_shape,
        scratch_shapes=scratch,
        compiler_params=pltpu.CompilerParams(vmem_limit_bytes=30 * MIB),
        cost_estimate=pl.CostEstimate(flops=1, bytes_accessed=1, transcendentals=0),
    )(*args)


def pack_kernel(tok_rows, index_ref, *refs):
    parts, late, out_ref, raw_ref = refs[:6], refs[6:8], refs[8], refs[9]
    rows, half = parts[0].shape
    wide = index_ref.shape[0]
    places = row_places(index_ref, tok_rows, 0, rows + late[0].shape[0])
    places = jnp.transpose(places.astype(F32)).astype(BF16)
    for j in range(2 * half // PIECE):
        side, at = j * PIECE // half, j * PIECE % half
        cols = slice(at, at + PIECE)
        summed = sum(p[:, cols].astype(F32) for p in parts[side::2])
        summed = jnp.concatenate([summed, late[side][:, cols].astype(F32)], axis=0)
        put_piece(raw_ref, j, wide, mul(places, summed.astype(BF16)))
    narrow_raw(raw_ref, out_ref)


def combine_kernel(weight_ref, raw_ref, rows_ref, out_ref, held_ref, wide_ref, sems):
    chunks, tok_rows, chunk = held_ref.shape
    experts = weight_ref.shape[1] // (2 * MOST)
    widen_raw(raw_ref, wide_ref)
    weight = weight_ref[...]
    copies = []
    for k in range(chunks):
        for j in range(chunk // PIECE):
            got = get_piece(wide_ref, k * (chunk // PIECE) + j, experts)
            branch = mul(weight, jnp.concatenate([got, got], axis=0))
            at = k * chunk + j * PIECE
            rows = rows_ref[:, at : at + PIECE].astype(F32)
            held_ref[k, :, j * PIECE : (j + 1) * PIECE] = (rows + branch).astype(BF16)
        part = out_ref.at[:, pl.ds(k * chunk, chunk)]
        copies.append(pltpu.make_async_copy(held_ref.at[k], part, sems.at[k]))
        copies[k].start()
    for copy in copies:
        copy.wait()


def along_y(x, step):
    n = lax.axis_size("narrow")
    return lax.ppermute(x, "narrow", [(i, (i + 2 * step) % n) for i in range(n)])


def around_y(first_row, rows, tok_rows, arrived, pick_index, own, sibling):
    total = arrived.shape[0]
    width = own[2].shape[1]
    vmem = pl.BlockSpec(memory_space=pltpu.VMEM)
    raw_f32 = pltpu.VMEM((PIECE // BLOCK, total + total // pick_index.shape[0], BLOCK), F32)
    half_shape = jax.ShapeDtypeStruct((rows, width // 2), BF16)
    x0 = pl.pallas_call(
        functools.partial(unpack_kernel, tok_rows, first_row),
        in_specs=[vmem] * 2,
        out_specs=[vmem, vmem],
        out_shape=[half_shape, half_shape],
        scratch_shapes=[raw_f32],
        compiler_params=pltpu.CompilerParams(vmem_limit_bytes=24 * MIB),
    )(pick_index, arrived)

    xm, xp = [along_y(x0[0], 1), None], [None, along_y(x0[1], -1)]
    xm[1] = along_y(x0[1], 1)
    xp[0] = along_y(x0[0], -1)
    x2 = (along_y(xm[0], 1), along_y(xp[1], -1))

    weights = (own[0], own[1], sibling[0], sibling[1], own[2], sibling[2])
    *p0, w0, w1, w2, w3, w4, w5 = expert([x0], weights, (F32, F32), hold=True)
    weights = (w0, w1, w2, w3, w4, w5)
    xp[0], xp[1], xm[0], xm[1] = lax.optimization_barrier((*xp, *xm, p0[0]))[:4]
    pp_a, pp_b, pm_a, pm_b = expert([xp, xm], weights, (F32, BF16, BF16, F32))
    x2 = lax.optimization_barrier((*x2, pp_b))[:2]
    p2 = expert([x2], weights, (BF16, BF16))
    got_mb = along_y(pp_b, 1)
    got_pa = along_y(pm_a, -1)
    from_m = along_y(p2[0], 1)
    from_p = along_y(p2[1], -1)
    from_m, got_mb, got_pa = lax.optimization_barrier((from_m, got_mb, got_pa))
    got_ma = along_y((pp_a + from_m.astype(F32)).astype(BF16), 1)
    got_pb = along_y((pm_b + from_p.astype(F32)).astype(BF16), -1)
    return p0[0], p0[1], got_ma, got_mb, got_pa, got_pb


def local(
    tokens, block_scales, pick_index, pick_gates, pick_counts, gate_weight, up_weight, down_weight
):
    tok_rows, width = tokens.shape
    n_wide = lax.axis_size("wide")
    n_narrow = lax.axis_size("narrow")
    other_core = [(i, i ^ 1) for i in range(n_narrow)]
    per = MOST * (width // PIECE)
    total = n_wide * per
    scales = block_scales.T
    chunk = 2 * PIECE
    chunks = width // chunk
    vmem = pl.BlockSpec(memory_space=pltpu.VMEM)
    anywhere = pl.BlockSpec(memory_space=pl.ANY)

    own = (gate_weight[0].T, up_weight[0].T, down_weight[0])
    sibling = tuple(lax.ppermute(v, "narrow", other_core) for v in own)

    raw_shape = jax.ShapeDtypeStruct((total, PIECE), BF16)
    raw_f32 = pltpu.VMEM((PIECE // BLOCK, total + per, BLOCK), F32)
    held = pltpu.VMEM((chunks, tok_rows, chunk), BF16)
    sems = pltpu.SemaphoreType.DMA((chunks,))
    outgoing, most = pl.pallas_call(
        dispatch_kernel,
        in_specs=[anywhere] * 3,
        out_specs=[vmem, vmem],
        out_shape=[raw_shape, jax.ShapeDtypeStruct((1, 1), I32)],
        scratch_shapes=[
            pltpu.VMEM(pick_index.shape, I32),
            pltpu.VMEM(scales.shape, F32),
            held,
            raw_f32,
            pltpu.SemaphoreType.DMA((chunks + 2,)),
        ],
        compiler_params=pltpu.CompilerParams(vmem_limit_bytes=56 * MIB),
    )(pick_index, scales, tokens)

    def exchange(raw):
        raw = raw.reshape(n_wide, per, PIECE)
        raw = lax.all_to_all(raw, "wide", split_axis=0, concat_axis=0, tiled=True)
        return raw.reshape(total, PIECE)

    slots = MOST * n_wide
    rows_out, weight = pl.pallas_call(
        prepare_kernel,
        in_specs=[vmem] * 5,
        out_specs=[vmem] * 2,
        out_shape=[
            jax.ShapeDtypeStruct((tok_rows, width), BF16),
            jax.ShapeDtypeStruct((tok_rows, 2 * slots), BF16),
        ],
        compiler_params=pltpu.CompilerParams(vmem_limit_bytes=24 * MIB),
    )(pick_index, pick_gates, pick_counts.reshape(1, tok_rows), scales, tokens)

    arrived = exchange(outgoing)
    arrived, weight = lax.optimization_barrier((arrived, weight))
    rows = slots * 3 // 4
    parts = around_y(0, rows, tok_rows, arrived, pick_index, own, sibling)

    def second(arrived):
        late = around_y(rows, slots - rows, tok_rows, arrived, pick_index, own, sibling)
        return [sum(p.astype(F32) for p in late[side::2]).astype(BF16) for side in (0, 1)]

    def none(arrived):
        return [jnp.zeros((slots - rows, width // 2), BF16)] * 2

    arrived, *parts = lax.optimization_barrier((arrived, *parts))
    late = lax.cond(most[0, 0] > rows, second, none, arrived)
    packed = pl.pallas_call(
        functools.partial(pack_kernel, tok_rows),
        in_specs=[vmem] * 9,
        out_specs=vmem,
        out_shape=raw_shape,
        scratch_shapes=[raw_f32],
        compiler_params=pltpu.CompilerParams(vmem_limit_bytes=32 * MIB),
    )(pick_index, *parts, *late)
    returned = exchange(packed)
    return pl.pallas_call(
        combine_kernel,
        in_specs=[vmem] * 3,
        out_specs=anywhere,
        out_shape=jax.ShapeDtypeStruct((tok_rows, width), BF16),
        scratch_shapes=[held, raw_f32, sems],
        compiler_params=pltpu.CompilerParams(vmem_limit_bytes=24 * MIB),
    )(weight, returned, rows_out)


def solution(mesh):
    return jax.shard_map(
        local,
        mesh=mesh,
        in_specs=(
            P(("wide", "narrow"), None),
            P(("wide", "narrow"), None),
            P(),
            P(),
            P(("wide", "narrow")),
            P("wide", None, "narrow"),
            P("wide", None, "narrow"),
            P("wide", "narrow", None),
        ),
        out_specs=P(("wide", "narrow"), None),
        check_vma=False,
    )
```
